256 devices in a mesh: ctx: 32 (over z, x_lo, core), section: 8 (over y, x_hi).
Axes of the slice: x: 4 (x_hi: 2, x_lo: 2; x = x_hi * 2 + x_lo), y: 4, z: 8, core: 2. Of those that a mesh axis runs over, the one named last changes fastest.
Arguments:
- queries: bfloat16 [8, 8192, 4608], P('section', 'ctx'), may hold values from -32 to 32
- latent_cache: bfloat16 [8, 576, 8192], P('section', None, 'ctx'), may hold values from -4 to 4
- doc_ids: int32 [8, 8192], P('section', 'ctx'), may hold values from 0 to 7, never falling along the last dimension, each value on 1 to 6144 neighbouring positions
- block_table: int32 [32, 32], replicated, may hold values 0 or 1
- w_uv: bfloat16 [8, 8, 512, 128], P('section'), may hold values from -0.5 to 0.5
Outputs:
- handed: bfloat16 [8, 8192, 1024], P('section', 'ctx')
The draws below stay inside these ranges and needn't reach their ends.
Inputs may be any that keep to these rules, and one draw needn't show every extreme that they name: `doc_ids`: along each layer's 8192 tokens the document ids never fall.
All inputs are finite; a program needn't handle non-finite values.
Results may differ from the reference program's by a relative error of at most 0.009.
Values may be sent and summed in bfloat16 or wider, within the bound.
No kernel may reach another device: no remote copies, remote signals or barrier semaphores. Data moves between devices by JAX's collectives and lax.ppermute only.
A program may use at most 64 MiB of HBM per device.

```python
import math
import jax
import jax.numpy as jnp
import numpy as np
from jax import lax

LAT = 512
ROPE = 64
VD = 128
HEADS = 8
TOK_DEV = 256
QK = 576
TOKENS = 8192
LAYERS = 8
N_CTX = 32


def shared_cache(key, pull):
    key_normal = jax.random.fold_in(key, 0)
    key_pick = jax.random.fold_in(key, 2)
    normal_part = jnp.clip(jax.random.normal(key_normal, (LAYERS, TOKENS, QK), jnp.float32), -4.0, 4.0)
    rows_all = normal_part
    positions = jnp.arange(TOKENS, dtype=jnp.int32)
    picked = jax.random.bernoulli(key_pick, 0.125, (LAYERS, TOKENS)) & (positions % 2 == 1)[None, :]
    following = jnp.roll(picked, -1, axis=1)
    latent_next = jnp.roll(rows_all[..., :LAT], -1, axis=1)
    mirrored = -jnp.flip(latent_next, axis=-1)
    use_mirror = following[..., None] & (pull > 0.0)
    latent_rows = jnp.where(use_mirror, mirrored, rows_all[..., :LAT])
    return jnp.concatenate([latent_rows, rows_all[..., LAT:]], axis=-1)


def draw_latent_cache(key, part):
    rows_all = shared_cache(key, 0.0)
    return jnp.transpose(rows_all, (0, 2, 1)).astype(jnp.bfloat16)


def draw_queries(key, part):
    key = jax.random.fold_in(key, 7)
    result_rows = jnp.clip(jax.random.normal(key, (LAYERS, TOKENS, HEADS, QK), jnp.float32) * 1.5, -8.0, 8.0)
    return result_rows.reshape(LAYERS, TOKENS, HEADS * QK).astype(jnp.bfloat16)


def place_ends(entries, stream_key, smallest, largest):
    spot = [jax.random.randint(jax.random.fold_in(stream_key, axis), (), 0, length) for axis, length in enumerate(entries.shape)]
    longest = entries.shape.index(max(entries.shape))
    neighbour = spot[:longest] + [(spot[longest] + 1) % entries.shape[longest]] + spot[longest + 1:]
    return entries.at[tuple(spot)].set(smallest).at[tuple(neighbour)].set(largest)


def steps_of(stream_key, dims, cuts, least, largest):
    factor_of, own = 1.0, jax.random.fold_in(stream_key, 6)
    for dim, parts in cuts:
        heights = jnp.exp(jax.random.uniform(jax.random.fold_in(own, dim), (parts,), jnp.float32, least / len(cuts), largest / len(cuts)))
        factor_of = factor_of * jnp.repeat(heights, dims[dim] // parts).reshape([-1 if axis == dim else 1 for axis in range(len(dims))])
    return factor_of


def split_up(count, total, reach, slope):
    loads = [(1 << 20) // math.isqrt(grade ** slope) + 1 for grade in range(2, count + 1)]
    rest, counts = total - reach - (count - 1), [1] * (count - 1)
    while rest > 0:
        candidates = [i for i in range(count - 1) if counts[i] < reach]
        pool, budget = sum([loads[i] for i in candidates]), rest
        for i in candidates:
            more = min(reach - counts[i], max(1, budget * loads[i] // pool), rest)
            counts[i] = counts[i] + more
            rest = rest - more
    return np.array([reach] + counts)


def uneven_parts(stream_key, count, total, reach, slope):
    if count == 2:
        one = jax.random.randint(stream_key, (), max(1, total - reach), min(reach, total - 1) + 1)
        return jnp.stack([one, total - one])
    lengths = jnp.asarray(split_up(count, total, reach, slope), jnp.int32)
    couples = (count - 1) // 2
    source_of, receiver = lengths[1:1 + 2 * couples:2], lengths[2:2 + 2 * couples:2]
    room = jnp.minimum(source_of - 1, reach - receiver)
    shifted = jax.random.randint(jax.random.fold_in(stream_key, 1), (couples,), 0, 1 << 20) % (room + 1)
    lengths = lengths.at[1:1 + 2 * couples:2].set(source_of - shifted).at[2:2 + 2 * couples:2].set(receiver + shifted)
    return lengths[jax.random.permutation(jax.random.fold_in(stream_key, 2), count)]


def normal_values(own_key, dims, scale, reach, cuts=(), kind=jnp.bfloat16):
    level = steps_of(own_key, dims, cuts, -0.22, 0.18) if cuts else 1.0
    values = jax.random.normal(own_key, dims, jnp.float32) * scale * level
    return jnp.minimum(jnp.maximum(values, -reach), reach).astype(kind)


def setup_inputs(seed: int = 0) -> dict:
    streams_of = jax.random.split(jax.random.key(seed), 6)
    queries = draw_queries(jax.random.fold_in(streams_of[5], 71), 0)
    latent_cache = draw_latent_cache(jax.random.fold_in(streams_of[5], 71), 0)
    doc_ids = jax.vmap(lambda own: jnp.searchsorted(jnp.cumsum(uneven_parts(own, N_CTX // 4, TOKENS, 3 * TOKENS // 4, 2)), jnp.arange(TOKENS), side="right"))(jax.random.split(streams_of[2], LAYERS)).reshape((LAYERS, TOKENS)).astype(jnp.int32)
    block_table = place_ends((jax.random.randint(streams_of[3], (N_CTX, N_CTX), 0, 4) < 3).astype(jnp.int32), jax.random.fold_in(streams_of[3], 1), 0, 1)
    w_uv = normal_values(streams_of[4], (LAYERS, HEADS, LAT, VD), (LAT // 4) ** -0.5, 0.5, ((0, 8),))
    return {"queries": queries, "latent_cache": latent_cache, "doc_ids": doc_ids, "block_table": block_table, "w_uv": w_uv}


very_low = -1e30


def attend_block(carried, query_rows, query_ids, query_block, table_row, cache_block, key_ids, key_start, latent_width, score_scale):
    tokens_q = query_ids.shape[0]
    heads_q = query_rows.shape[0] // tokens_q
    key_count = cache_block.shape[1]
    key_block = key_start // tokens_q
    table_hit = jnp.sum(jnp.where(jnp.arange(table_row.shape[0], dtype=jnp.int32) == key_block, table_row, 0))
    opened = (table_hit == 1) | (key_block == query_block)
    is_live = (key_block == query_block) | ((key_block < query_block) & (table_hit == 1) & (key_ids[-1] >= query_ids[0]))

    def compute(current):
        peak_old, total_old, accum_old = current
        scores = jnp.dot(query_rows, cache_block, preferred_element_type=jnp.float32) * score_scale
        scores = scores.reshape(tokens_q, heads_q, key_count)
        query_pos = query_block * tokens_q + jnp.arange(tokens_q, dtype=jnp.int32)
        key_pos = key_start + jnp.arange(key_count, dtype=jnp.int32)
        allowed = (query_ids[:, None] == key_ids[None, :]) & (key_pos[None, :] <= query_pos[:, None]) & opened
        allowed = allowed[:, None, :]
        scores = jnp.where(allowed, scores, very_low)
        peak_new = jnp.maximum(peak_old, jnp.max(scores, axis=2))
        weights = jnp.where(allowed, jnp.exp(scores - peak_new[:, :, None]), 0.0)
        factor = jnp.exp(peak_old - peak_new)
        total_new = total_old * factor + jnp.sum(weights, axis=2)
        weights_low = weights.astype(jnp.bfloat16).reshape(tokens_q * heads_q, key_count)
        values = cache_block[:latent_width]
        mixed_part = lax.dot_general(weights_low, values, (((1,), (1,)), ((), ())), preferred_element_type=jnp.float32)
        accum_new = accum_old * factor.reshape(-1, 1) + mixed_part
        return peak_new, total_new, accum_new

    return lax.cond(is_live, compute, lambda current: current, carried)


def finish(final_state, weights_uv):
    row_peak, row_total, row_accum = final_state
    tokens_q, heads_q = row_total.shape
    mixed_rows = (row_accum / row_total.reshape(-1, 1)).astype(jnp.bfloat16).reshape(tokens_q, heads_q, -1)
    projected = jnp.einsum("thl,hlv->thv", mixed_rows.astype(jnp.float32), weights_uv.astype(jnp.float32))
    return projected.reshape(tokens_q, -1).astype(jnp.bfloat16)


def reference(queries, latent_cache, doc_ids, block_table, w_uv):
    score_scale = (VD + ROPE) ** -0.5
    outputs = []
    for layer_index in range(LAYERS):
        layer_queries = queries[layer_index]
        layer_cache = latent_cache[layer_index]
        layer_ids = doc_ids[layer_index]
        layer_weights = w_uv[layer_index]

        def one_block(query_block):
            query_rows = lax.dynamic_slice_in_dim(layer_queries, query_block * TOK_DEV, TOK_DEV, 0).reshape(TOK_DEV * HEADS, QK)
            query_ids = lax.dynamic_slice_in_dim(layer_ids, query_block * TOK_DEV, TOK_DEV, 0)
            table_row = block_table[query_block]
            initial = (jnp.full((TOK_DEV, HEADS), very_low, jnp.float32), jnp.zeros((TOK_DEV, HEADS), jnp.float32), jnp.zeros((TOK_DEV * HEADS, LAT), jnp.float32))

            def over_keys(carried, key_block):
                key_start = (key_block * TOK_DEV).astype(jnp.int32)
                cache_block = lax.dynamic_slice_in_dim(layer_cache, key_start, TOK_DEV, 1)
                key_ids = lax.dynamic_slice_in_dim(layer_ids, key_start, TOK_DEV, 0)
                return attend_block(carried, query_rows, query_ids, query_block, table_row, cache_block, key_ids, key_start, LAT, score_scale), None

            final_state, unused = lax.scan(over_keys, initial, jnp.arange(N_CTX, dtype=jnp.int32))
            return finish(final_state, layer_weights)

        blocks = lax.map(one_block, jnp.arange(N_CTX, dtype=jnp.int32))
        outputs.append(blocks.reshape(TOKENS, HEADS * VD))
    stacked = jnp.stack(outputs)
    return jnp.roll(stacked, 1, axis=0)
```

```python
import functools
import jax
import jax.numpy as jnp
from jax import lax
from jax.experimental import pallas as pl
from jax.experimental.pallas import tpu as pltpu
from jax.sharding import PartitionSpec as P

very_low = -1e30
log2_e = 1.4426950408889634
id_rows = 16
documents = 8


def dot(a, b, of_a, of_b):
    return lax.dot_general(a, b, (((of_a,), (of_b,)), ((), ())), preferred_element_type=jnp.float32)


def attend(places, first, final, factor_scale, ids_s, table, ids_v, queries, *refs):
    count = len(places)
    blocks, refs = refs[:count], refs[count:]
    if final:
        up, refs = refs[0], refs[1:]
    if not first:
        refs = refs[3:]
    (peak, total, accum), refs = refs[:3], refs[3:]
    if final:
        out, refs = refs[0], refs[1:]
    flipped, values, bias, score_buf, weight_buf, factor_buf = refs
    heads, latent, tokens = accum.shape
    width = queries.shape[0] // heads
    me = lax.axis_index("ctx")
    if first:
        peak[...] = jnp.full(peak.shape, very_low, jnp.float32)
        total[...] = jnp.zeros(total.shape, jnp.float32)
        accum[...] = jnp.zeros(accum.shape, jnp.float32)
    weight_buf[1] = jnp.zeros(weight_buf.shape[1:], weight_buf.dtype)
    factor_buf[1] = jnp.ones(factor_buf.shape[1:], factor_buf.dtype)
    first_id = ids_s[0, 0]
    query_ids = ids_v[...]
    key_at = lax.broadcasted_iota(jnp.int32, (tokens, tokens), 0)
    live_count = jnp.int32(0)
    for j, (back, flip) in enumerate(places):
        block = blocks[j]
        origin = (me ^ flip) - 4 * back
        key_ids = block[width : width + id_rows, :].astype(jnp.float32)[0:1, :]
        before = jnp.sum(jnp.where(key_ids < first_id.astype(jnp.float32), 1.0, 0.0)).astype(jnp.int32)
        if back == 0 and flip == 0:
            live = jnp.bool_(True)
        else:
            hit = table[me, jnp.maximum(origin, 0)]
            live = (origin >= 0) & (origin < me) & (hit == 1) & (before < tokens)

        def pack(block=block, key_ids=key_ids, before=before, slot=live_count, own=back == 0 and flip == 0):
            flipped[slot] = block[0:width, :].T
            values[slot] = block[0:latent, :]
            if own:
                start = jnp.zeros(query_ids.shape, jnp.int32)
                for d in range(documents):
                    below = jnp.sum(jnp.where(key_ids < float(d), 1.0, 0.0), axis=1, keepdims=True)
                    start = jnp.where(query_ids == d, below.astype(jnp.int32), start)
                query_at = lax.broadcasted_iota(jnp.int32, (tokens, tokens), 1)
                allowed = (key_at >= start) & (key_at <= query_at)
            else:
                allowed = (key_at >= before) & (query_ids == first_id)
            bias[slot] = jnp.where(allowed, 0.0, very_low)

        if back == 0 and flip == 0:
            pack()
        else:
            pl.when(live)(pack)
        live_count = live_count + live.astype(jnp.int32)

    def score(slot, head, half):
        rows = queries[head * width : (head + 1) * width, :]
        score_buf[half] = dot(flipped[slot], rows, 1, 0) + bias[slot]

    def weigh(head, half):
        scores = score_buf[half]
        old = peak[head : head + 1, :]
        new = jnp.maximum(old, jnp.max(scores, axis=0, keepdims=True))
        factor = jnp.exp2((old - new) * factor_scale)
        weights = jnp.exp2((scores - new) * factor_scale)
        total[head : head + 1, :] = total[head : head + 1, :] * factor + jnp.sum(weights, axis=0, keepdims=True)
        peak[head : head + 1, :] = new
        factor_buf[half] = jnp.broadcast_to(factor, factor_buf.shape[1:])
        weight_buf[half] = weights.astype(jnp.bfloat16)

    def mix(slot, head, half):
        accum[head] = accum[head] * factor_buf[half][0:1, :] + dot(values[slot], weight_buf[half], 1, 0)

    @pl.when(live_count > 0)
    def _():
        score(0, 0, 0)

        def over_live(slot, carry):
            after, prior = jnp.minimum(slot + 1, live_count - 1), jnp.maximum(slot - 1, 0)
            for head in range(heads):
                half = head % 2
                score(slot if head < heads - 1 else after, (head + 1) % heads, 1 - half)
                weigh(head, half)
                mix(slot if head > 0 else prior, (head - 1) % heads, 1 - half)
            return carry

        lax.fori_loop(0, live_count, over_live, 0)
        mix(live_count - 1, heads - 1, (heads - 1) % 2)

    if final:
        value_width = up.shape[2]
        for head in range(heads):
            mixed = (accum[head] / total[head : head + 1, :]).astype(jnp.bfloat16)
            part = dot(up[head], mixed, 0, 0)
            out[:, head * value_width : (head + 1) * value_width] = part.T.astype(jnp.bfloat16)


def stage(places, blocks, ids, table, queries, state, up, sizes):
    heads, latent, tokens, width, value_width = sizes
    first, final = state is None, up is not None
    count = len(places)
    scalars, vectors = pl.BlockSpec(memory_space=pltpu.SMEM), pl.BlockSpec(memory_space=pltpu.VMEM)
    shapes = [((heads, tokens), jnp.float32), ((heads, tokens), jnp.float32), ((heads, latent, tokens), jnp.float32)]
    operands = [ids, table, ids, queries, *blocks]
    specs = [scalars, scalars, vectors, vectors] + [vectors] * count
    aliases = {}
    if final:
        operands.append(up)
        specs.append(vectors)
    out_shape = [pltpu.VMEM(shape, dtype) for shape, dtype in shapes]
    if final:
        out_shape.append(jax.ShapeDtypeStruct((tokens, heads * value_width), jnp.bfloat16))
    if not first:
        aliases = {len(operands) + i: i for i in range(3)}
        operands += [pltpu.with_memory_space_constraint(x, pltpu.VMEM) for x in state]
        specs += [vectors] * 3
    scratch = [
        pltpu.VMEM((count, tokens, width), jnp.bfloat16),
        pltpu.VMEM((count, latent, tokens), jnp.bfloat16),
        pltpu.VMEM((count, tokens, tokens), jnp.float32),
        pltpu.VMEM((2, tokens, tokens), jnp.float32),
        pltpu.VMEM((2, tokens, tokens), jnp.bfloat16),
        pltpu.VMEM((2, 8, tokens), jnp.float32),
    ]
    scale = (value_width + width - latent) ** -0.5 * log2_e
    work = 2 * count * heads * tokens * tokens * (width + latent)
    result = pl.pallas_call(
        functools.partial(attend, tuple(places), first, final, scale),
        out_shape=out_shape,
        in_specs=specs,
        out_specs=[vectors] * len(out_shape),
        scratch_shapes=scratch,
        input_output_aliases=aliases,
        cost_estimate=pl.CostEstimate(
            flops=work, bytes_accessed=count * 2 * width * tokens, transcendentals=count * heads * tokens * tokens
        ),
        compiler_params=pltpu.CompilerParams(vmem_limit_bytes=24 * 2**20),
        name="attend",
    )(*operands)
    return result[3] if final else result


def shards(queries, latent_cache, doc_ids, block_table, w_uv):
    tokens, heads, latent, value_width = queries.shape[1], w_uv.shape[1], w_uv.shape[2], w_uv.shape[3]
    width = latent_cache.shape[1]
    sizes = (heads, latent, tokens, width, value_width)
    devices = lax.axis_size("ctx")
    planes = devices // 4

    def send(x, to, least=0):
        pairs = [(i, to(i)) for i in range(devices)]
        return lax.ppermute(x, "ctx", [(i, o) for i, o in pairs if least <= o // 4 and 0 <= o < devices])

    across = lambda x, least=0: send(x, lambda i: i ^ 2, least)
    core = lambda x, least=0: send(x, lambda i: i ^ 1, least)
    up_one = lambda x, least: send(x, lambda i: i + 4, least)

    ids = jnp.broadcast_to(doc_ids.astype(jnp.bfloat16), (id_rows, tokens))
    own = jnp.concatenate([latent_cache[0], ids], axis=0)
    turned = queries[0].T
    queries_t = pltpu.with_memory_space_constraint(turned, pltpu.VMEM)

    def run(places, blocks, state, up=None):
        return stage(places, blocks, doc_ids, block_table, queries_t, state, up, sizes)

    ups, far = {0: own}, {}
    across_of, core_of, core_across_of = {}, {}, {}
    core_of[0], across_of[0] = core(own), across(own)
    ups[1] = up_one(own, 1)
    ups[6] = send(own, lambda i: i + 24)
    ups[5] = send(own, lambda i: i + 20)
    state = run([(0, 0), (0, 1)], [own, core_of[0]], None)
    for k in (1, 2, 3, 4):
        if k < 4:
            ups[k + 1] = up_one(ups[k], k + 1)
        across_of[k], core_of[k] = across(ups[k], k), core(ups[k], k)
        core_across_of[k - 1] = core(across_of[k - 1], k - 1)
        places = [(k - 1, 2), (k - 1, 3), (k, 0), (k, 1)]
        blocks = [across_of[k - 1], core_across_of[k - 1], ups[k], core_of[k]]
        if k == 4:
            for far in (5, 6):
                core_of[far], across_of[far] = core(ups[far], far), across(ups[far], far)
                places += [(far, 0), (far, 1)]
                blocks += [ups[far], core_of[far]]
        state = run(places, blocks, state)
    places, blocks = [], []
    for k in (4, 5, 6):
        core_across_of[k] = core(across_of[k], k)
        places += [(k, 2), (k, 3)]
        blocks += [across_of[k], core_across_of[k]]
    heads_out = run(places, blocks, state, w_uv[0])
    sections = lax.axis_size("section")
    return lax.ppermute(heads_out[None], "section", [(i, (i + 1) % sections) for i in range(sections)])


def solution(mesh):
    placed = (
        P("section", "ctx", None),
        P("section", None, "ctx"),
        P("section", "ctx"),
        P(),
        P("section", None, None, None),
    )
    return jax.shard_map(
        shards, mesh=mesh, in_specs=placed, out_specs=P("section", "ctx", None), check_vma=False
    )
```

```python
import functools
import jax
import jax.numpy as jnp
from jax import lax
from jax.experimental import pallas as pl
from jax.experimental.pallas import tpu as pltpu
from jax.sharding import PartitionSpec as P

very_low = -1e30
log2_e = 1.4426950408889634
id_rows = 16
documents = 8


def dot(a, b, of_a, of_b):
    return lax.dot_general(a, b, (((of_a,), (of_b,)), ((), ())), preferred_element_type=jnp.float32)


def origin_of(me, place, e):
    step, across, swapped = place
    holder = me ^ (2 * across + swapped)
    if step == 0:
        return holder ^ e
    back = jnp.where((holder & 1) == 0, step, 7 - step)
    return (holder ^ e) - 4 * back


def attend(places, first, final, factor_scale, info, ids_v, queries, *refs):
    pieces, refs = refs[: len(places)], refs[len(places) :]
    if final:
        up, refs = refs[0], refs[1:]
    if not first:
        refs = refs[3:]
    (peak, total, accum), refs = refs[:3], refs[3:]
    if final:
        out, refs = refs[0], refs[1:]
    flipped, values, bias, score_buf, weight_buf, factor_buf = refs
    heads, latent, tokens = accum.shape
    width = queries.shape[0] // heads
    me = info[0, 0]
    first_id = info[0, 1]
    blocks = []
    for piece, place in zip(pieces, places):
        for e in range(piece.shape[0]):
            blocks.append((piece.at[e], place, e))
    if first:
        peak[...] = jnp.full(peak.shape, very_low, jnp.float32)
        total[...] = jnp.zeros(total.shape, jnp.float32)
        accum[...] = jnp.zeros(accum.shape, jnp.float32)
    query_ids = ids_v[...]
    key_at = lax.broadcasted_iota(jnp.int32, (tokens, tokens), 0)
    first_float = first_id.astype(jnp.float32)
    key_ids = [b[width : width + id_rows, :].astype(jnp.float32)[0:1, :] for b, _, _ in blocks]
    counts = [jnp.sum(jnp.where(k < first_float, 1.0, 0.0), axis=1, keepdims=True) for k in key_ids]
    befores = [c[0, 0].astype(jnp.int32) for c in counts]
    live_count = jnp.int32(0)
    for (block, place, e), ids_here, before in zip(blocks, key_ids, befores):
        own = place == (0, 0, 0) and e == 0
        origin = origin_of(me, place, e)
        if own:
            live = jnp.bool_(True)
        else:
            hit = info[0, 2 + jnp.maximum(origin, 0)]
            live = (origin >= 0) & (origin < me) & (hit == 1) & (before < tokens)

        def pack(block=block, ids_here=ids_here, before=before, slot=live_count, own=own):
            flipped[slot] = block[0:width, :].T
            values[slot] = block[0:latent, :]
            if own:
                start = jnp.zeros(query_ids.shape, jnp.int32)
                for d in range(documents):
                    below = jnp.sum(jnp.where(ids_here < float(d), 1.0, 0.0), axis=1, keepdims=True)
                    start = jnp.where(query_ids == d, below.astype(jnp.int32), start)
                query_at = lax.broadcasted_iota(jnp.int32, (tokens, tokens), 1)
                allowed = (key_at >= start) & (key_at <= query_at)
            else:
                allowed = (key_at >= before) & (query_ids == first_id)
            bias[slot] = jnp.where(allowed, 0.0, very_low)

        if own:
            pack()
        else:
            pl.when(live)(pack)
        live_count = live_count + live.astype(jnp.int32)

    def score(slot, head, half):
        rows = queries[head * width : (head + 1) * width, :]
        score_buf[half] = dot(flipped[slot], rows, 1, 0) + bias[slot]

    def weigh(head, half):
        scores = score_buf[half]
        old = peak[head : head + 1, :]
        new = jnp.maximum(old, jnp.max(scores, axis=0, keepdims=True))
        factor = jnp.exp2((old - new) * factor_scale)
        weights = jnp.exp2((scores - new) * factor_scale)
        total[head : head + 1, :] = total[head : head + 1, :] * factor + jnp.sum(weights, axis=0, keepdims=True)
        peak[head : head + 1, :] = new
        factor_buf[half] = jnp.broadcast_to(factor, factor_buf.shape[1:])
        weight_buf[half] = weights.astype(jnp.bfloat16)

    def mix(slot, head, half):
        accum[head] = accum[head] * factor_buf[half][0:1, :] + dot(values[slot], weight_buf[half], 1, 0)

    @pl.when(live_count > 0)
    def _():
        weight_buf[1] = jnp.zeros(weight_buf.shape[1:], weight_buf.dtype)
        factor_buf[1] = jnp.ones(factor_buf.shape[1:], factor_buf.dtype)
        score(0, 0, 0)

        def over_live(slot, carry):
            after, prior = jnp.minimum(slot + 1, live_count - 1), jnp.maximum(slot - 1, 0)
            for head in range(heads):
                half = head % 2
                score(slot if head < heads - 1 else after, (head + 1) % heads, 1 - half)
                weigh(head, half)
                mix(slot if head > 0 else prior, (head - 1) % heads, 1 - half)
            return carry

        lax.fori_loop(0, live_count, over_live, 0)
        mix(live_count - 1, heads - 1, (heads - 1) % 2)

    if final:
        value_width = up.shape[2]
        for head in range(heads):
            mixed = (accum[head] / total[head : head + 1, :]).astype(jnp.bfloat16)
            part = dot(up[head], mixed, 0, 0)
            out[:, head * value_width : (head + 1) * value_width] = part.T.astype(jnp.bfloat16)


def stage(places, pieces, info, ids, queries, state, up, sizes):
    heads, latent, tokens, width, value_width = sizes
    first, final = state is None, up is not None
    count = sum(p.shape[0] for p in pieces)
    scalars, vectors = pl.BlockSpec(memory_space=pltpu.SMEM), pl.BlockSpec(memory_space=pltpu.VMEM)
    shapes = [((heads, tokens), jnp.float32), ((heads, tokens), jnp.float32), ((heads, latent, tokens), jnp.float32)]
    operands = [info, ids, queries, *pieces]
    specs = [scalars, vectors, vectors] + [vectors] * len(pieces)
    aliases = {}
    out_shape = [pltpu.VMEM(shape, dtype) for shape, dtype in shapes]
    if final:
        operands.append(up)
        specs.append(vectors)
        out_shape.append(jax.ShapeDtypeStruct((tokens, heads * value_width), jnp.bfloat16))
    if not first:
        aliases = {len(operands) + i: i for i in range(3)}
        operands += [pltpu.with_memory_space_constraint(x, pltpu.VMEM) for x in state]
        specs += [vectors] * 3
    scratch = [
        pltpu.VMEM((count, tokens, width), jnp.bfloat16),
        pltpu.VMEM((count, latent, tokens), jnp.bfloat16),
        pltpu.VMEM((count, tokens, tokens), jnp.float32),
        pltpu.VMEM((2, tokens, tokens), jnp.float32),
        pltpu.VMEM((2, tokens, tokens), jnp.bfloat16),
        pltpu.VMEM((2, 8, tokens), jnp.float32),
    ]
    scale = (value_width + width - latent) ** -0.5 * log2_e
    work = 2 * count * heads * tokens * tokens * (width + latent)
    result = pl.pallas_call(
        functools.partial(attend, tuple(places), first, final, scale),
        out_shape=out_shape,
        in_specs=specs,
        out_specs=[vectors] * len(out_shape),
        scratch_shapes=scratch,
        input_output_aliases=aliases,
        cost_estimate=pl.CostEstimate(
            flops=work, bytes_accessed=count * 2 * width * tokens, transcendentals=count * heads * tokens * tokens
        ),
        compiler_params=pltpu.CompilerParams(vmem_limit_bytes=24 * 2**20),
        name="attend",
    )(*operands)
    return result[3] if final else list(result)


def tie(*arrays):
    return list(lax.optimization_barrier(tuple(arrays)))


def shards(queries, latent_cache, doc_ids, block_table, w_uv):
    tokens, heads, latent, value_width = queries.shape[1], w_uv.shape[1], w_uv.shape[2], w_uv.shape[3]
    width = latent_cache.shape[1]
    sizes = (heads, latent, tokens, width, value_width)
    devices = lax.axis_size("ctx")
    planes = devices // 4
    me = lax.axis_index("ctx")

    def across(x, step=0):
        return lax.ppermute(x, "ctx", [(i, i ^ 2) for i in range(devices) if i // 4 >= least(step, i % 2)])

    def core(x, step=0):
        return lax.ppermute(x, "ctx", [(i, i ^ 1) for i in range(devices) if i // 4 >= least(step, i % 2)])

    def least(step, odd):
        return 0 if step == 0 else step if odd == 0 else planes - 1 - step

    def along(x, step):
        pairs = []
        for i in range(devices):
            plane = i // 4
            if i % 2 == 0:
                if step - 1 <= plane < planes - 1:
                    pairs.append((i, i + 4))
            else:
                source = (plane + step) % planes if step > 1 else plane
                if source < planes // 2:
                    pairs.append((i, (i - (8 if step == 1 else 4)) % devices))
        return lax.ppermute(x, "ctx", pairs)

    ids = jnp.broadcast_to(doc_ids.astype(jnp.bfloat16), (id_rows, tokens))
    own = jnp.concatenate([latent_cache[0], ids], axis=0)[None]
    c0, x0 = core(own), across(own)
    row = lax.dynamic_slice_in_dim(block_table, me, 1, 0)
    info = jnp.concatenate([jnp.full((1, 1), me, jnp.int32), doc_ids[:, :1], row], axis=1)
    queries_t = pltpu.with_memory_space_constraint(queries[0].T, pltpu.VMEM)

    def run(places, pieces, state, up=None):
        return stage(places, pieces, info, doc_ids, queries_t, state, up, sizes)

    pair = jnp.concatenate([own, c0], axis=0)
    z1 = along(pair, 1)
    cx0 = core(x0)
    state = run([(0, 0, 0)], [pair], None)
    state = run([(0, 1, 0), (0, 1, 1)], [x0, cx0], state)
    z2, x1 = along(z1, 2), across(z1, 1)
    *state, z1 = tie(*state, z1)
    state = run([(1, 0, 0)], [z1], state)
    *state, z1, z2 = tie(*state, z1, z2)
    cz1 = core(z1, 1)
    z3 = along(z2, 3)
    state = run([(1, 0, 1)], [cz1], state)
    *state, z2, x1 = tie(*state, z2, x1)
    x2 = across(z2, 2)
    state = run([(1, 1, 0)], [x1], state)
    *state, x1, z3 = tie(*state, x1, z3)
    cx1 = core(x1, 1)
    state = run([(2, 0, 0)], [z2], state)
    *state, z3, cx1 = tie(*state, z3, cx1)
    x3 = across(z3, 3)
    state = run([(1, 1, 1)], [cx1], state)
    *state, z2 = tie(*state, z2)
    cz2 = core(z2, 2)
    state = run([(3, 0, 0)], [z3], state)
    *state, z3, cz2 = tie(*state, z3, cz2)
    cz3 = core(z3, 3)
    state = run([(2, 0, 1)], [cz2], state)
    *state, x2, cz3 = tie(*state, x2, cz3)
    cx2 = core(x2, 2)
    state = run([(2, 1, 0), (3, 0, 1)], [x2, cz3], state)
    *state, x3, cx2 = tie(*state, x3, cx2)
    cx3 = core(x3, 3)
    state = run([(2, 1, 1), (3, 1, 0)], [cx2, x3], state)
    heads_out = run([(3, 1, 1)], [cx3], state, w_uv[0])
    sections = lax.axis_size("section")
    return lax.ppermute(heads_out[None], "section", [(i, (i + 1) % sections) for i in range(sections)])


def solution(mesh):
    placed = (
        P("section", "ctx", None),
        P("section", None, "ctx"),
        P("section", "ctx"),
        P(),
        P("section", None, None, None),
    )
    return jax.shard_map(
        shards, mesh=mesh, in_specs=placed, out_specs=P("section", "ctx", None), check_vma=False
    )
```

```python
import functools
import jax
import jax.numpy as jnp
from jax import lax
from jax.experimental import pallas as pl
from jax.experimental.pallas import tpu as pltpu
from jax.sharding import PartitionSpec as P

very_low = -1e30
log2_e = 1.4426950408889634
id_rows = 16
documents = 8


def dot(a, b, of_a, of_b):
    return lax.dot_general(a, b, (((of_a,), (of_b,)), ((), ())), preferred_element_type=jnp.float32)


def origin_of(me, place, e):
    step, across, swapped = place
    holder = me ^ (2 * across + swapped)
    if step == 0:
        return holder ^ e
    back = jnp.where((holder & 1) == 0, step, 7 - step)
    return (holder ^ e) - 4 * back


def attend(places, first, final, factor_scale, info, ids_v, queries, *refs):
    pieces, refs = refs[: len(places)], refs[len(places) :]
    if final:
        up, refs = refs[0], refs[1:]
    if not first:
        refs = refs[3:]
    (peak, total, accum), refs = refs[:3], refs[3:]
    if final:
        out, refs = refs[0], refs[1:]
    flipped, values, bias, score_buf, weight_buf, factor_buf = refs
    heads, latent, tokens = accum.shape
    width = queries.shape[0] // heads
    me = info[0, 0]
    first_id = info[0, 1]
    blocks = []
    for piece, place in zip(pieces, places):
        for e in range(piece.shape[0]):
            blocks.append((piece.at[e], place, e))
    if first:
        peak[...] = jnp.full(peak.shape, very_low, jnp.float32)
        total[...] = jnp.zeros(total.shape, jnp.float32)
        accum[...] = jnp.zeros(accum.shape, jnp.float32)
    query_ids = ids_v[...]
    key_at = lax.broadcasted_iota(jnp.int32, (tokens, tokens), 0)
    first_float = first_id.astype(jnp.float32)
    key_ids = [b[width : width + id_rows, :].astype(jnp.float32)[0:1, :] for b, _, _ in blocks]
    counts = [jnp.sum(jnp.where(k < first_float, 1.0, 0.0), axis=1, keepdims=True) for k in key_ids]
    befores = [c[0, 0].astype(jnp.int32) for c in counts]
    live_count = jnp.int32(0)
    for (block, place, e), ids_here, before in zip(blocks, key_ids, befores):
        own = place == (0, 0, 0) and e == 0
        origin = origin_of(me, place, e)
        if own:
            live = jnp.bool_(True)
        else:
            hit = info[0, 2 + jnp.maximum(origin, 0)]
            live = (origin >= 0) & (origin < me) & (hit == 1) & (before < tokens)

        def pack(block=block, ids_here=ids_here, before=before, slot=live_count, own=own):
            flipped[slot] = block[0:width, :].T
            values[slot] = block[0:latent, :]
            if own:
                start = jnp.zeros(query_ids.shape, jnp.int32)
                for d in range(documents):
                    below = jnp.sum(jnp.where(ids_here < float(d), 1.0, 0.0), axis=1, keepdims=True)
                    start = jnp.where(query_ids == d, below.astype(jnp.int32), start)
                query_at = lax.broadcasted_iota(jnp.int32, (tokens, tokens), 1)
                allowed = (key_at >= start) & (key_at <= query_at)
            else:
                allowed = (key_at >= before) & (query_ids == first_id)
            bias[slot] = jnp.where(allowed, 0.0, very_low)

        if own:
            pack()
        else:
            pl.when(live)(pack)
        live_count = live_count + live.astype(jnp.int32)

    def score(slot, head, half):
        rows = queries[head * width : (head + 1) * width, :]
        score_buf[half] = dot(flipped[slot], rows, 1, 0) + bias[slot]

    def weigh(head, half):
        scores = score_buf[half]
        old = peak[head : head + 1, :]
        new = jnp.maximum(old, jnp.max(scores, axis=0, keepdims=True))
        factor = jnp.exp2((old - new) * factor_scale)
        weights = jnp.exp2((scores - new) * factor_scale)
        total[head : head + 1, :] = total[head : head + 1, :] * factor + jnp.sum(weights, axis=0, keepdims=True)
        peak[head : head + 1, :] = new
        factor_buf[half] = jnp.broadcast_to(factor, factor_buf.shape[1:])
        weight_buf[half] = weights.astype(jnp.bfloat16)

    def mix(slot, head, half):
        accum[head] = accum[head] * factor_buf[half][0:1, :] + dot(values[slot], weight_buf[half], 1, 0)

    @pl.when(live_count > 0)
    def _():
        weight_buf[1] = jnp.zeros(weight_buf.shape[1:], weight_buf.dtype)
        factor_buf[1] = jnp.ones(factor_buf.shape[1:], factor_buf.dtype)
        score(0, 0, 0)

        def over_live(slot, carry):
            after, prior = jnp.minimum(slot + 1, live_count - 1), jnp.maximum(slot - 1, 0)
            for head in range(heads):
                half = head % 2
                score(slot if head < heads - 1 else after, (head + 1) % heads, 1 - half)
                weigh(head, half)
                mix(slot if head > 0 else prior, (head - 1) % heads, 1 - half)
            return carry

        lax.fori_loop(0, live_count, over_live, 0)
        mix(live_count - 1, heads - 1, (heads - 1) % 2)

    if final:
        value_width = up.shape[2]
        for head in range(heads):
            mixed = (accum[head] / total[head : head + 1, :]).astype(jnp.bfloat16)
            part = dot(up[head], mixed, 0, 0)
            out[:, head * value_width : (head + 1) * value_width] = part.T.astype(jnp.bfloat16)


def stage(places, pieces, info, ids, queries, state, up, sizes):
    heads, latent, tokens, width, value_width = sizes
    first, final = state is None, up is not None
    count = sum(p.shape[0] for p in pieces)
    scalars, vectors = pl.BlockSpec(memory_space=pltpu.SMEM), pl.BlockSpec(memory_space=pltpu.VMEM)
    shapes = [((heads, tokens), jnp.float32), ((heads, tokens), jnp.float32), ((heads, latent, tokens), jnp.float32)]
    operands = [info, ids, queries, *pieces]
    specs = [scalars, vectors, vectors] + [vectors] * len(pieces)
    aliases = {}
    out_shape = [pltpu.VMEM(shape, dtype) for shape, dtype in shapes]
    if final:
        operands.append(up)
        specs.append(vectors)
        out_shape.append(jax.ShapeDtypeStruct((tokens, heads * value_width), jnp.bfloat16))
    if not first:
        aliases = {len(operands) + i: i for i in range(3)}
        operands += [pltpu.with_memory_space_constraint(x, pltpu.VMEM) for x in state]
        specs += [vectors] * 3
    scratch = [
        pltpu.VMEM((count, tokens, width), jnp.bfloat16),
        pltpu.VMEM((count, latent, tokens), jnp.bfloat16),
        pltpu.VMEM((count, tokens, tokens), jnp.float32),
        pltpu.VMEM((2, tokens, tokens), jnp.float32),
        pltpu.VMEM((2, tokens, tokens), jnp.bfloat16),
        pltpu.VMEM((2, 8, tokens), jnp.float32),
    ]
    scale = (value_width + width - latent) ** -0.5 * log2_e
    work = 2 * count * heads * tokens * tokens * (width + latent)
    result = pl.pallas_call(
        functools.partial(attend, tuple(places), first, final, scale),
        out_shape=out_shape,
        in_specs=specs,
        out_specs=[vectors] * len(out_shape),
        scratch_shapes=scratch,
        input_output_aliases=aliases,
        cost_estimate=pl.CostEstimate(
            flops=work, bytes_accessed=count * 2 * width * tokens, transcendentals=count * heads * tokens * tokens
        ),
        compiler_params=pltpu.CompilerParams(vmem_limit_bytes=24 * 2**20),
        name="attend",
    )(*operands)
    return result[3] if final else list(result)


def tie(*arrays):
    return list(lax.optimization_barrier(tuple(arrays)))


def shards(queries, latent_cache, doc_ids, block_table, w_uv):
    tokens, heads, latent, value_width = queries.shape[1], w_uv.shape[1], w_uv.shape[2], w_uv.shape[3]
    width = latent_cache.shape[1]
    sizes = (heads, latent, tokens, width, value_width)
    devices = lax.axis_size("ctx")
    me = lax.axis_index("ctx")

    def across(x):
        return lax.ppermute(x, "ctx", [(i, i ^ 2) for i in range(devices)])

    def core(x):
        return lax.ppermute(x, "ctx", [(i, i ^ 1) for i in range(devices)])

    def along(x, step):
        down = 8 if step == 1 else 4
        return lax.ppermute(x, "ctx", [(i, (i + 4 if i % 2 == 0 else i - down) % devices) for i in range(devices)])

    ids = jnp.broadcast_to(doc_ids.astype(jnp.bfloat16), (id_rows, tokens))
    own = jnp.concatenate([latent_cache[0], ids], axis=0)[None]
    c0, x0 = core(own), across(own)
    row = lax.dynamic_slice_in_dim(block_table, me, 1, 0)
    info = jnp.concatenate([jnp.full((1, 1), me, jnp.int32), doc_ids[:, :1], row], axis=1)
    queries_t = pltpu.with_memory_space_constraint(queries[0].T, pltpu.VMEM)

    def run(places, pieces, state, up=None):
        return stage(places, pieces, info, doc_ids, queries_t, state, up, sizes)

    pair = jnp.concatenate([own, c0], axis=0)
    z1 = along(pair, 1)
    cx0 = core(x0)
    state = run([(0, 0, 0)], [pair], None)
    *state, z1 = tie(*state, z1)
    z2, cz1, x1 = along(z1, 2), core(z1), across(z1)
    state = run([(0, 1, 0), (0, 1, 1)], [x0, cx0], state)
    *state, z2 = tie(*state, z2)
    z3, cz2 = along(z2, 3), core(z2)
    state = run([(1, 0, 0), (1, 0, 1)], [z1, cz1], state)
    *state, x1 = tie(*state, x1)
    xz2, cx1 = along(x1, 2), core(x1)
    state = run([(2, 0, 0), (2, 0, 1)], [z2, cz2], state)
    *state, z3 = tie(*state, z3)
    x3, cz3 = across(z3), core(z3)
    state = run([(1, 1, 0), (1, 1, 1)], [x1, cx1], state)
    *state, xz2 = tie(*state, xz2)
    cxz2 = core(xz2)
    state = run([(3, 0, 0), (3, 0, 1)], [z3, cz3], state)
    *state, x3 = tie(*state, x3)
    cx3 = core(x3)
    state = run([(2, 1, 0), (2, 1, 1)], [xz2, cxz2], state)
    heads_out = run([(3, 1, 0), (3, 1, 1)], [x3, cx3], state, w_uv[0])
    sections = lax.axis_size("section")
    return lax.ppermute(heads_out[None], "section", [(i, (i + 1) % sections) for i in range(sections)])


def solution(mesh):
    placed = (
        P("section", "ctx", None),
        P("section", None, "ctx"),
        P("section", "ctx"),
        P(),
        P("section", None, None, None),
    )
    return jax.shard_map(
        shards, mesh=mesh, in_specs=placed, out_specs=P("section", "ctx", None), check_vma=False
    )
```

```python
import functools
import jax
import jax.numpy as jnp
from jax import lax
from jax.experimental import pallas as pl
from jax.experimental.pallas import tpu as pltpu
from jax.sharding import PartitionSpec as P

very_low = -1e30
log2_e = 1.4426950408889634
id_rows = 16
documents = 8


def dot(a, b, of_a, of_b):
    return lax.dot_general(a, b, (((of_a,), (of_b,)), ((), ())), preferred_element_type=jnp.float32)


def origin_of(me, place, e):
    step, across, swapped = place
    holder = me ^ (2 * across + swapped)
    if step == 0:
        return holder ^ e
    back = jnp.where((holder & 1) == 0, step, 7 - step)
    return (holder ^ e) - 4 * back


def attend(places, first, chosen, final, factor_scale, row, ids_s, ids_v, queries, *refs):
    pieces, refs = refs[: len(places)], refs[len(places) :]
    if final:
        up, refs = refs[0], refs[1:]
    if not first:
        refs = refs[3:]
    (peak, total, accum), refs = refs[:3], refs[3:]
    if final:
        out, refs = refs[0], refs[1:]
    flipped, turned, values, bias, score_buf, weight_buf, factor_buf = refs
    heads, latent, tokens = accum.shape
    width = queries.shape[0] // heads
    me = lax.axis_index("ctx")
    first_id = ids_s[0, 0]
    blocks = []
    for piece, place in zip(pieces, places):
        for e in range(piece.shape[0]):
            blocks.append((piece.at[e], place, e))
    if first:
        peak[...] = jnp.full(peak.shape, very_low, jnp.float32)
        total[...] = jnp.zeros(total.shape, jnp.float32)
        accum[...] = jnp.zeros(accum.shape, jnp.float32)
    query_ids = ids_v[...]
    key_at = lax.broadcasted_iota(jnp.int32, (tokens, tokens), 0)
    first_float = first_id.astype(jnp.float32)
    key_ids = [b[width : width + id_rows, :].astype(jnp.float32)[0:1, :] for b, _, _ in blocks]
    counts = [jnp.sum(jnp.where(k < first_float, 1.0, 0.0), axis=1, keepdims=True) for k in key_ids]
    befores = [c[0, 0].astype(jnp.int32) for c in counts]
    live_count = jnp.int32(0)
    for (block, place, e), ids_here, before in zip(blocks, key_ids, befores):
        own = place == (0, 0, 0) and e == 0
        origin = origin_of(me, place, e)
        if own:
            live = jnp.bool_(True)
        else:
            hit = row[0, jnp.maximum(origin, 0)]
            live = (origin >= 0) & (origin < me) & (hit == 1) & (before < tokens)

        def pack(block=block, ids_here=ids_here, before=before, slot=live_count, own=own):
            values[slot] = block[0:width, :]
            if own:
                start = jnp.zeros(query_ids.shape, jnp.int32)
                for d in range(documents):
                    below = jnp.sum(jnp.where(ids_here < float(d), 1.0, 0.0), axis=1, keepdims=True)
                    start = jnp.where(query_ids == d, below.astype(jnp.int32), start)
                query_at = lax.broadcasted_iota(jnp.int32, (tokens, tokens), 1)
                allowed = (key_at >= start) & (key_at <= query_at)
            else:
                allowed = (key_at >= before) & (query_ids == first_id)
            bias[slot] = jnp.where(allowed, 0.0, very_low)

        if own:
            pack()
        else:
            pl.when(live)(pack)
        live_count = live_count + live.astype(jnp.int32)

    spans = [slice(at, min(at + 128, width)) for at in range(0, width, 128)]
    count = len(chosen)
    shares = [spans[len(spans) * i // (count - 1) : len(spans) * (i + 1) // (count - 1)] for i in range(count - 1)]

    def score(slot, head, half):
        rows = queries[head * width : (head + 1) * width, :]
        score_buf[half] = dot(flipped[...], rows, 1, 0) + bias[slot]

    def weigh(head, half):
        scores = score_buf[half]
        old = peak[head : head + 1, :]
        new = jnp.maximum(old, jnp.max(scores, axis=0, keepdims=True))
        factor = jnp.exp2((old - new) * factor_scale)
        weights = jnp.exp2((scores - new) * factor_scale)
        total[head : head + 1, :] = total[head : head + 1, :] * factor + jnp.sum(weights, axis=0, keepdims=True)
        peak[head : head + 1, :] = new
        factor_buf[half] = jnp.broadcast_to(factor, factor_buf.shape[1:])
        weight_buf[half] = weights.astype(jnp.bfloat16)

    def mix(slot, head, half):
        accum[head] = accum[head] * factor_buf[half][0:1, :] + dot(values[slot, 0:latent, :], weight_buf[half], 1, 0)

    @pl.when(live_count > 0)
    def _():
        weight_buf[1] = jnp.zeros(weight_buf.shape[1:], weight_buf.dtype)
        factor_buf[1] = jnp.ones(factor_buf.shape[1:], factor_buf.dtype)
        flipped[...] = values[0].T
        score(0, chosen[0], 0)

        def over_live(slot, carry):
            after, prior = jnp.minimum(slot + 1, live_count - 1), jnp.maximum(slot - 1, 0)
            for i, head in enumerate(chosen):
                half = i % 2
                if i == count - 1:
                    flipped[...] = turned[...]
                score(slot if i < count - 1 else after, chosen[(i + 1) % count], 1 - half)
                weigh(head, half)
                mix(slot if i > 0 else prior, chosen[i - 1], 1 - half)
                if i < count - 1:
                    for span in shares[i]:
                        turned[:, span] = values[after, span, :].T
            return carry

        lax.fori_loop(0, live_count, over_live, 0)
        mix(live_count - 1, chosen[-1], (count - 1) % 2)

    if final:
        value_width = up.shape[2]
        for i, head in enumerate(chosen):
            mixed = (accum[head] / total[head : head + 1, :]).astype(jnp.bfloat16)
            part = dot(up[head], mixed, 0, 0)
            out[:, i * value_width : (i + 1) * value_width] = part.T.astype(jnp.bfloat16)


def stage(places, pieces, row, ids, queries, state, up, sizes, chosen=None):
    heads, latent, tokens, width, value_width = sizes
    first, final = state is None, up is not None
    chosen = tuple(range(heads)) if chosen is None else chosen
    count = sum(p.shape[0] for p in pieces)
    scalars, vectors = pl.BlockSpec(memory_space=pltpu.SMEM), pl.BlockSpec(memory_space=pltpu.VMEM)
    shapes = [((heads, tokens), jnp.float32), ((heads, tokens), jnp.float32), ((heads, latent, tokens), jnp.float32)]
    operands = [row, ids, ids, queries, *pieces]
    specs = [scalars, scalars, vectors, vectors] + [vectors] * len(pieces)
    aliases = {}
    out_shape = [pltpu.VMEM(shape, dtype) for shape, dtype in shapes]
    if final:
        operands.append(up)
        specs.append(vectors)
        out_shape.append(jax.ShapeDtypeStruct((tokens, len(chosen) * value_width), jnp.bfloat16))
    if not first:
        aliases = {len(operands) + i: i for i in range(3)}
        operands += [pltpu.with_memory_space_constraint(x, pltpu.VMEM) for x in state]
        specs += [vectors] * 3
    scratch = [
        pltpu.VMEM((tokens, width), jnp.bfloat16),
        pltpu.VMEM((tokens, width), jnp.bfloat16),
        pltpu.VMEM((count, width, tokens), jnp.bfloat16),
        pltpu.VMEM((count, tokens, tokens), jnp.float32),
        pltpu.VMEM((2, tokens, tokens), jnp.float32),
        pltpu.VMEM((2, tokens, tokens), jnp.bfloat16),
        pltpu.VMEM((2, 8, tokens), jnp.float32),
    ]
    scale = (value_width + width - latent) ** -0.5 * log2_e
    work = 2 * count * heads * tokens * tokens * (width + latent)
    result = pl.pallas_call(
        functools.partial(attend, tuple(places), first, chosen, final, scale),
        out_shape=out_shape,
        in_specs=specs,
        out_specs=[vectors] * len(out_shape),
        scratch_shapes=scratch,
        input_output_aliases=aliases,
        cost_estimate=pl.CostEstimate(
            flops=work, bytes_accessed=count * 2 * width * tokens, transcendentals=count * heads * tokens * tokens
        ),
        compiler_params=pltpu.CompilerParams(vmem_limit_bytes=24 * 2**20),
        name="attend",
    )(*operands)
    return list(result)


def tie(*arrays):
    return list(lax.optimization_barrier(tuple(arrays)))


def shards(queries, latent_cache, doc_ids, block_table, w_uv):
    tokens, heads, latent, value_width = queries.shape[1], w_uv.shape[1], w_uv.shape[2], w_uv.shape[3]
    width = latent_cache.shape[1]
    sizes = (heads, latent, tokens, width, value_width)
    devices = lax.axis_size("ctx")
    me = lax.axis_index("ctx")

    def across(x):
        return lax.ppermute(x, "ctx", [(i, i ^ 2) for i in range(devices)])

    def core(x):
        return lax.ppermute(x, "ctx", [(i, i ^ 1) for i in range(devices)])

    def along(x, step):
        down = 8 if step == 1 else 4
        return lax.ppermute(x, "ctx", [(i, (i + 4 if i % 2 == 0 else i - down) % devices) for i in range(devices)])

    ids = jnp.broadcast_to(doc_ids.astype(jnp.bfloat16), (id_rows, tokens))
    own = jnp.concatenate([latent_cache[0], ids], axis=0)[None]
    c0, x0 = core(own), across(own)
    row = lax.dynamic_slice_in_dim(block_table, me, 1, 0)

    pair = jnp.concatenate([own, c0], axis=0)
    z1 = along(pair, 1)
    queries_t = pltpu.with_memory_space_constraint(queries[0].T, pltpu.VMEM)

    def run(places, pieces, state, up=None, chosen=None):
        return stage(places, pieces, row, doc_ids, queries_t, state, up, sizes, chosen)

    state = run([(0, 0, 0)], [pair], None)
    *state, x0 = tie(*state, x0)
    cx0 = core(x0)
    state = run([(0, 1, 0)], [x0], state)
    *state, z1 = tie(*state, z1)
    z2, cz1, x1 = along(z1, 2), core(z1), across(z1)
    state = run([(0, 1, 1), (1, 0, 0)], [cx0, z1], state)
    *state, z2 = tie(*state, z2)
    z3, cz2 = along(z2, 3), core(z2)
    state = run([(1, 0, 1), (2, 0, 0)], [cz1, z2], state)
    *state, x1, z3 = tie(*state, x1, z3)
    x3, xz2, cx1, cz3 = across(z3), along(x1, 2), core(x1), core(z3)
    state = run([(2, 0, 1), (1, 1, 0)], [cz2, x1], state)
    state = run([(1, 1, 1), (3, 0, 0)], [cx1, z3], state)
    *state, xz2, x3 = tie(*state, xz2, x3)
    cxz2, cx3 = core(xz2), core(x3)
    state = run([(3, 0, 1)], [cz3], state)
    sections = lax.axis_size("section")
    handed = []
    for part in (tuple(range(heads - heads // 4)), tuple(range(heads - heads // 4, heads))):
        *state, heads_out = run(
            [(2, 1, 0), (2, 1, 1), (3, 1, 0), (3, 1, 1)], [xz2, cxz2, x3, cx3], state, w_uv[0], part
        )
        handed.append(lax.ppermute(heads_out[None], "section", [(i, (i + 1) % sections) for i in range(sections)]))
    return jnp.concatenate(handed, axis=2)


def solution(mesh):
    placed = (
        P("section", "ctx", None),
        P("section", None, "ctx"),
        P("section", "ctx"),
        P(),
        P("section", None, None, None),
    )
    return jax.shard_map(
        shards, mesh=mesh, in_specs=placed, out_specs=P("section", "ctx", None), check_vma=False
    )
```

```python
import functools
import jax
import jax.numpy as jnp
from jax import lax
from jax.experimental import pallas as pl
from jax.experimental.pallas import tpu as pltpu
from jax.sharding import PartitionSpec as P

very_low = -1e30
log2_e = 1.4426950408889634
id_rows = 16
documents = 8


def dot(a, b, of_a, of_b):
    return lax.dot_general(a, b, (((of_a,), (of_b,)), ((), ())), preferred_element_type=jnp.float32)


def origin_of(me, place, e):
    step, across, swapped = place
    holder = me ^ (2 * across + swapped)
    if step == 0:
        return holder ^ e
    back = jnp.where((holder & 1) == 0, step, 7 - step)
    return (holder ^ e) - 4 * back


def attend(places, first, chosen, final, factor_scale, row, ids_s, ids_v, queries, *refs):
    pieces, refs = refs[: len(places)], refs[len(places) :]
    if final:
        up, refs = refs[0], refs[1:]
    if not first:
        refs = refs[3:]
    (peak, total, accum), refs = refs[:3], refs[3:]
    if final:
        out, refs = refs[0], refs[1:]
    flipped, turned, values, bias, score_buf, weight_buf, factor_buf = refs
    heads, latent, tokens = accum.shape
    width = queries.shape[0] // heads
    me = lax.axis_index("ctx")
    first_id = ids_s[0, 0]
    blocks = []
    for piece, place in zip(pieces, places):
        for e in range(piece.shape[0]):
            blocks.append((piece.at[e], place, e))
    if first:
        peak[...] = jnp.full(peak.shape, very_low, jnp.float32)
        total[...] = jnp.zeros(total.shape, jnp.float32)
        accum[...] = jnp.zeros(accum.shape, jnp.float32)
    query_ids = ids_v[...]
    key_at = lax.broadcasted_iota(jnp.int32, (tokens, tokens), 0)
    first_float = first_id.astype(jnp.float32)
    key_ids = [b[width : width + id_rows, :].astype(jnp.float32)[0:1, :] for b, _, _ in blocks]
    counts = [jnp.sum(jnp.where(k < first_float, 1.0, 0.0), axis=1, keepdims=True) for k in key_ids]
    befores = [c[0, 0].astype(jnp.int32) for c in counts]
    live_count = jnp.int32(0)
    for (block, place, e), ids_here, before in zip(blocks, key_ids, befores):
        own = place == (0, 0, 0) and e == 0
        origin = origin_of(me, place, e)
        if own:
            live = jnp.bool_(True)
        else:
            hit = row[0, jnp.maximum(origin, 0)]
            live = (origin >= 0) & (origin < me) & (hit == 1) & (before < tokens)

        def pack(block=block, ids_here=ids_here, before=before, slot=live_count, own=own):
            values[slot] = block[0:width, :]
            if own:
                start = jnp.zeros(query_ids.shape, jnp.int32)
                for d in range(documents):
                    below = jnp.sum(jnp.where(ids_here < float(d), 1.0, 0.0), axis=1, keepdims=True)
                    start = jnp.where(query_ids == d, below.astype(jnp.int32), start)
                query_at = lax.broadcasted_iota(jnp.int32, (tokens, tokens), 1)
                allowed = (key_at >= start) & (key_at <= query_at)
            else:
                allowed = (key_at >= before) & (query_ids == first_id)
            bias[slot] = jnp.where(allowed, 0.0, very_low)

        if own:
            pack()
        else:
            pl.when(live)(pack)
        live_count = live_count + live.astype(jnp.int32)

    spans = [slice(at, min(at + 128, width)) for at in range(0, width, 128)]
    count = len(chosen)
    shares = [spans[len(spans) * i // (count - 1) : len(spans) * (i + 1) // (count - 1)] for i in range(count - 1)]

    def score(slot, head, half):
        rows = queries[head * width : (head + 1) * width, :]
        score_buf[half] = dot(flipped[...], rows, 1, 0) + bias[slot]

    def weigh(head, half):
        scores = score_buf[half]
        old = peak[head : head + 1, :]
        new = jnp.maximum(old, jnp.max(scores, axis=0, keepdims=True))
        factor = jnp.exp2((old - new) * factor_scale)
        weights = jnp.exp2((scores - new) * factor_scale)
        total[head : head + 1, :] = total[head : head + 1, :] * factor + jnp.sum(weights, axis=0, keepdims=True)
        peak[head : head + 1, :] = new
        factor_buf[half] = jnp.broadcast_to(factor, factor_buf.shape[1:])
        weight_buf[half] = weights.astype(jnp.bfloat16)

    def mix(slot, head, half):
        accum[head] = accum[head] * factor_buf[half][0:1, :] + dot(values[slot, 0:latent, :], weight_buf[half], 1, 0)

    @pl.when(live_count > 0)
    def _():
        weight_buf[1] = jnp.zeros(weight_buf.shape[1:], weight_buf.dtype)
        factor_buf[1] = jnp.ones(factor_buf.shape[1:], factor_buf.dtype)
        flipped[...] = values[0].T
        score(0, chosen[0], 0)

        def over_live(slot, carry):
            after, prior = jnp.minimum(slot + 1, live_count - 1), jnp.maximum(slot - 1, 0)
            for i, head in enumerate(chosen):
                half = i % 2
                if i == count - 1:
                    flipped[...] = turned[...]
                score(slot if i < count - 1 else after, chosen[(i + 1) % count], 1 - half)
                weigh(head, half)
                mix(slot if i > 0 else prior, chosen[i - 1], 1 - half)
                if i < count - 1:
                    for span in shares[i]:
                        turned[:, span] = values[after, span, :].T
            return carry

        lax.fori_loop(0, live_count, over_live, 0)
        mix(live_count - 1, chosen[-1], (count - 1) % 2)

    if final:
        value_width = up.shape[2]
        for i, head in enumerate(chosen):
            mixed = (accum[head] / total[head : head + 1, :]).astype(jnp.bfloat16)
            part = dot(up[head], mixed, 0, 0)
            out[:, i * value_width : (i + 1) * value_width] = part.T.astype(jnp.bfloat16)


def stage(places, pieces, row, ids, queries, state, up, sizes, chosen=None):
    heads, latent, tokens, width, value_width = sizes
    first, final = state is None, up is not None
    chosen = tuple(range(heads)) if chosen is None else chosen
    count = sum(p.shape[0] for p in pieces)
    scalars, vectors = pl.BlockSpec(memory_space=pltpu.SMEM), pl.BlockSpec(memory_space=pltpu.VMEM)
    shapes = [((heads, tokens), jnp.float32), ((heads, tokens), jnp.float32), ((heads, latent, tokens), jnp.float32)]
    operands = [row, ids, ids, queries, *pieces]
    specs = [scalars, scalars, vectors, vectors] + [vectors] * len(pieces)
    aliases = {}
    out_shape = [pltpu.VMEM(shape, dtype) for shape, dtype in shapes]
    if final:
        operands.append(up)
        specs.append(vectors)
        out_shape.append(jax.ShapeDtypeStruct((tokens, len(chosen) * value_width), jnp.bfloat16))
    if not first:
        aliases = {len(operands) + i: i for i in range(3)}
        operands += [pltpu.with_memory_space_constraint(x, pltpu.VMEM) for x in state]
        specs += [vectors] * 3
    scratch = [
        pltpu.VMEM((tokens, width), jnp.bfloat16),
        pltpu.VMEM((tokens, width), jnp.bfloat16),
        pltpu.VMEM((count, width, tokens), jnp.bfloat16),
        pltpu.VMEM((count, tokens, tokens), jnp.float32),
        pltpu.VMEM((2, tokens, tokens), jnp.float32),
        pltpu.VMEM((2, tokens, tokens), jnp.bfloat16),
        pltpu.VMEM((2, 8, tokens), jnp.float32),
    ]
    scale = (value_width + width - latent) ** -0.5 * log2_e
    work = 2 * count * heads * tokens * tokens * (width + latent)
    result = pl.pallas_call(
        functools.partial(attend, tuple(places), first, chosen, final, scale),
        out_shape=out_shape,
        in_specs=specs,
        out_specs=[vectors] * len(out_shape),
        scratch_shapes=scratch,
        input_output_aliases=aliases,
        cost_estimate=pl.CostEstimate(
            flops=work, bytes_accessed=count * 2 * width * tokens, transcendentals=count * heads * tokens * tokens
        ),
        compiler_params=pltpu.CompilerParams(vmem_limit_bytes=24 * 2**20),
        name="attend",
    )(*operands)
    return list(result)


def tie(*arrays):
    return list(lax.optimization_barrier(tuple(arrays)))


def shards(queries, latent_cache, doc_ids, block_table, w_uv):
    tokens, heads, latent, value_width = queries.shape[1], w_uv.shape[1], w_uv.shape[2], w_uv.shape[3]
    width = latent_cache.shape[1]
    sizes = (heads, latent, tokens, width, value_width)
    devices = lax.axis_size("ctx")
    me = lax.axis_index("ctx")

    def across(x):
        return lax.ppermute(x, "ctx", [(i, i ^ 2) for i in range(devices)])

    def core(x):
        return lax.ppermute(x, "ctx", [(i, i ^ 1) for i in range(devices)])

    def along(x, step):
        down = 8 if step == 1 else 4
        return lax.ppermute(x, "ctx", [(i, (i + 4 if i % 2 == 0 else i - down) % devices) for i in range(devices)])

    ids = jnp.broadcast_to(doc_ids.astype(jnp.bfloat16), (id_rows, tokens))
    own = jnp.concatenate([latent_cache[0], ids], axis=0)[None]
    c0, x0 = core(own), across(own)
    row = lax.dynamic_slice_in_dim(block_table, me, 1, 0)

    pair = jnp.concatenate([own, c0], axis=0)
    z1 = along(pair, 1)
    queries_t = pltpu.with_memory_space_constraint(queries[0].T, pltpu.VMEM)

    def run(places, pieces, state, up=None, chosen=None):
        return stage(places, pieces, row, doc_ids, queries_t, state, up, sizes, chosen)

    state = run([(0, 0, 0)], [pair], None)
    *state, x0 = tie(*state, x0)
    cx0 = core(x0)
    state = run([(0, 1, 0)], [x0], state)
    *state, z1 = tie(*state, z1)
    z2, cz1, x1 = along(z1, 2), core(z1), across(z1)
    state = run([(0, 1, 1), (1, 0, 0)], [cx0, z1], state)
    *state, z2 = tie(*state, z2)
    z3, cz2 = along(z2, 3), core(z2)
    state = run([(1, 0, 1), (2, 0, 0)], [cz1, z2], state)
    *state, x1, z3 = tie(*state, x1, z3)
    x3, xz2, cx1, cz3 = across(z3), along(x1, 2), core(x1), core(z3)
    state = run([(2, 0, 1), (1, 1, 0), (3, 0, 0)], [cz2, x1, z3], state)
    *state, xz2, x3 = tie(*state, xz2, x3)
    cxz2, cx3 = core(xz2), core(x3)
    state = run([(1, 1, 1), (3, 0, 1), (2, 1, 0)], [cx1, cz3, xz2], state)
    sections = lax.axis_size("section")
    handed = []
    for part in (tuple(range(heads - heads // 4)), tuple(range(heads - heads // 4, heads))):
        *state, heads_out = run(
            [(2, 1, 1), (3, 1, 0), (3, 1, 1)], [cxz2, x3, cx3], state, w_uv[0], part
        )
        handed.append(lax.ppermute(heads_out[None], "section", [(i, (i + 1) % sections) for i in range(sections)]))
    return jnp.concatenate(handed, axis=2)


def solution(mesh):
    placed = (
        P("section", "ctx", None),
        P("section", None, "ctx"),
        P("section", "ctx"),
        P(),
        P("section", None, None, None),
    )
    return jax.shard_map(
        shards, mesh=mesh, in_specs=placed, out_specs=P("section", "ctx", None), check_vma=False
    )
```

```python
import functools
import jax
import jax.numpy as jnp
from jax import lax
from jax.experimental import pallas as pl
from jax.experimental.pallas import tpu as pltpu
from jax.sharding import PartitionSpec as P

very_low = -1e30
log2_e = 1.4426950408889634
id_rows = 16
documents = 8


def dot(a, b, of_a, of_b):
    return lax.dot_general(a, b, (((of_a,), (of_b,)), ((), ())), preferred_element_type=jnp.float32)


def origin_of(me, place, e):
    step, across, swapped = place
    holder = me ^ (2 * across + swapped)
    if step == 0:
        return holder ^ e
    back = jnp.where((holder & 1) == 0, step, 7 - step)
    return (holder ^ e) - 4 * back


def attend(places, first, chosen, final, factor_scale, row, ids_s, ids_v, queries, *refs):
    pieces, refs = refs[: len(places)], refs[len(places) :]
    if final:
        up, refs = refs[0], refs[1:]
    if not first:
        refs = refs[3:]
    (peak, total, accum), refs = refs[:3], refs[3:]
    if final:
        out, refs = refs[0], refs[1:]
    flipped, turned, values, bias, score_buf, weight_buf, factor_buf = refs
    heads, latent, tokens = accum.shape
    width = queries.shape[0] // heads
    me = lax.axis_index("ctx")
    first_id = ids_s[0, 0]
    blocks = []
    for piece, place in zip(pieces, places):
        for e in range(piece.shape[0]):
            blocks.append((piece.at[e], place, e))
    if first:
        peak[...] = jnp.full(peak.shape, very_low, jnp.float32)
        total[...] = jnp.zeros(total.shape, jnp.float32)
        accum[...] = jnp.zeros(accum.shape, jnp.float32)
    query_ids = ids_v[...]
    key_at = lax.broadcasted_iota(jnp.int32, (tokens, tokens), 0)
    first_float = first_id.astype(jnp.float32)
    key_ids = [b[width : width + id_rows, :].astype(jnp.float32)[0:1, :] for b, _, _ in blocks]
    counts = [jnp.sum(jnp.where(k < first_float, 1.0, 0.0), axis=1, keepdims=True) for k in key_ids]
    befores = [c[0, 0].astype(jnp.int32) for c in counts]
    live_count = jnp.int32(0)
    for (block, place, e), ids_here, before in zip(blocks, key_ids, befores):
        own = place == (0, 0, 0) and e == 0
        origin = origin_of(me, place, e)
        if own:
            live = jnp.bool_(True)
        else:
            hit = row[0, jnp.maximum(origin, 0)]
            live = (origin >= 0) & (origin < me) & (hit == 1) & (before < tokens)

        def pack(block=block, ids_here=ids_here, before=before, slot=live_count, own=own):
            values[slot] = block[0:width, :]
            if own:
                start = jnp.zeros(query_ids.shape, jnp.int32)
                for d in range(documents):
                    below = jnp.sum(jnp.where(ids_here < float(d), 1.0, 0.0), axis=1, keepdims=True)
                    start = jnp.where(query_ids == d, below.astype(jnp.int32), start)
                query_at = lax.broadcasted_iota(jnp.int32, (tokens, tokens), 1)
                allowed = (key_at >= start) & (key_at <= query_at)
            else:
                allowed = (key_at >= before) & (query_ids == first_id)
            bias[slot] = jnp.where(allowed, 0.0, very_low)

        if own:
            pack()
        else:
            pl.when(live)(pack)
        live_count = live_count + live.astype(jnp.int32)

    spans = [slice(at, min(at + 128, width)) for at in range(0, width, 128)]
    count = len(chosen)
    shares = [spans[len(spans) * i // (count - 1) : len(spans) * (i + 1) // (count - 1)] for i in range(count - 1)]

    def score(slot, head, half):
        rows = queries[head * width : (head + 1) * width, :]
        score_buf[half] = dot(flipped[...], rows, 1, 0) + bias[slot]

    def weigh(head, half):
        scores = score_buf[half]
        old = peak[head : head + 1, :]
        new = jnp.maximum(old, jnp.max(scores, axis=0, keepdims=True))
        factor = jnp.exp2((old - new) * factor_scale)
        weights = jnp.exp2((scores - new) * factor_scale)
        total[head : head + 1, :] = total[head : head + 1, :] * factor + jnp.sum(weights, axis=0, keepdims=True)
        peak[head : head + 1, :] = new
        factor_buf[half] = jnp.broadcast_to(factor, factor_buf.shape[1:])
        weight_buf[half] = weights.astype(jnp.bfloat16)

    def mix(slot, head, half):
        accum[head] = accum[head] * factor_buf[half][0:1, :] + dot(values[slot, 0:latent, :], weight_buf[half], 1, 0)

    @pl.when(live_count > 0)
    def _():
        weight_buf[1] = jnp.zeros(weight_buf.shape[1:], weight_buf.dtype)
        factor_buf[1] = jnp.ones(factor_buf.shape[1:], factor_buf.dtype)
        flipped[...] = values[0].T
        score(0, chosen[0], 0)

        def over_live(slot, carry):
            after, prior = jnp.minimum(slot + 1, live_count - 1), jnp.maximum(slot - 1, 0)
            for i, head in enumerate(chosen):
                half = i % 2
                if i == count - 1:
                    flipped[...] = turned[...]
                score(slot if i < count - 1 else after, chosen[(i + 1) % count], 1 - half)
                weigh(head, half)
                mix(slot if i > 0 else prior, chosen[i - 1], 1 - half)
                if i < count - 1:
                    for span in shares[i]:
                        turned[:, span] = values[after, span, :].T
            return carry

        lax.fori_loop(0, live_count, over_live, 0)
        mix(live_count - 1, chosen[-1], (count - 1) % 2)

    if final:
        value_width = up.shape[2]
        for i, head in enumerate(chosen):
            mixed = (accum[head] / total[head : head + 1, :]).astype(jnp.bfloat16)
            part = dot(up[head], mixed, 0, 0)
            out[:, i * value_width : (i + 1) * value_width] = part.T.astype(jnp.bfloat16)


def stage(places, pieces, row, ids, queries, state, up, sizes, chosen=None):
    heads, latent, tokens, width, value_width = sizes
    first, final = state is None, up is not None
    chosen = tuple(range(heads)) if chosen is None else chosen
    count = sum(p.shape[0] for p in pieces)
    scalars, vectors = pl.BlockSpec(memory_space=pltpu.SMEM), pl.BlockSpec(memory_space=pltpu.VMEM)
    shapes = [((heads, tokens), jnp.float32), ((heads, tokens), jnp.float32), ((heads, latent, tokens), jnp.float32)]
    operands = [row, ids, ids, queries, *pieces]
    specs = [scalars, scalars, vectors, vectors] + [vectors] * len(pieces)
    aliases = {}
    out_shape = [pltpu.VMEM(shape, dtype) for shape, dtype in shapes]
    if final:
        operands.append(up)
        specs.append(vectors)
        out_shape.append(jax.ShapeDtypeStruct((tokens, len(chosen) * value_width), jnp.bfloat16))
    if not first:
        aliases = {len(operands) + i: i for i in range(3)}
        operands += [pltpu.with_memory_space_constraint(x, pltpu.VMEM) for x in state]
        specs += [vectors] * 3
    scratch = [
        pltpu.VMEM((tokens, width), jnp.bfloat16),
        pltpu.VMEM((tokens, width), jnp.bfloat16),
        pltpu.VMEM((count, width, tokens), jnp.bfloat16),
        pltpu.VMEM((count, tokens, tokens), jnp.float32),
        pltpu.VMEM((2, tokens, tokens), jnp.float32),
        pltpu.VMEM((2, tokens, tokens), jnp.bfloat16),
        pltpu.VMEM((2, 8, tokens), jnp.float32),
    ]
    scale = (value_width + width - latent) ** -0.5 * log2_e
    work = 2 * count * heads * tokens * tokens * (width + latent)
    result = pl.pallas_call(
        functools.partial(attend, tuple(places), first, chosen, final, scale),
        out_shape=out_shape,
        in_specs=specs,
        out_specs=[vectors] * len(out_shape),
        scratch_shapes=scratch,
        input_output_aliases=aliases,
        cost_estimate=pl.CostEstimate(
            flops=work, bytes_accessed=count * 2 * width * tokens, transcendentals=count * heads * tokens * tokens
        ),
        compiler_params=pltpu.CompilerParams(vmem_limit_bytes=24 * 2**20),
        name="attend",
    )(*operands)
    return list(result)


def join(cache, ids, own, pair):
    width = cache.shape[1]
    rows = jnp.broadcast_to(ids[...].astype(jnp.float32), (id_rows, ids.shape[1])).astype(jnp.bfloat16)
    for out in (own, pair):
        out[0, 0:width, :] = cache[0]
        out[0, width : width + id_rows, :] = rows


def fill(other, half, pair):
    pair[1] = other[0]


def in_vmem(kernel, out_shape, operands, aliases):
    vectors = pl.BlockSpec(memory_space=pltpu.VMEM)
    return pl.pallas_call(
        kernel,
        out_shape=out_shape,
        in_specs=[vectors] * len(operands),
        out_specs=[vectors] * len(out_shape),
        input_output_aliases=aliases,
        compiler_params=pltpu.CompilerParams(vmem_limit_bytes=8 * 2**20),
    )(*operands)


def tie(*arrays):
    return list(lax.optimization_barrier(tuple(arrays)))


def shards(queries, latent_cache, doc_ids, block_table, w_uv):
    tokens, heads, latent, value_width = queries.shape[1], w_uv.shape[1], w_uv.shape[2], w_uv.shape[3]
    width = latent_cache.shape[1]
    sizes = (heads, latent, tokens, width, value_width)
    devices = lax.axis_size("ctx")
    me = lax.axis_index("ctx")

    def across(x):
        return lax.ppermute(x, "ctx", [(i, i ^ 2) for i in range(devices)])

    def core(x):
        return lax.ppermute(x, "ctx", [(i, i ^ 1) for i in range(devices)])

    def along(x, step):
        down = 8 if step == 1 else 4
        return lax.ppermute(x, "ctx", [(i, (i + 4 if i % 2 == 0 else i - down) % devices) for i in range(devices)])

    rows = width + id_rows
    own, half = in_vmem(
        join,
        [pltpu.VMEM((1, rows, tokens), jnp.bfloat16), pltpu.VMEM((2, rows, tokens), jnp.bfloat16)],
        [latent_cache, doc_ids],
        {},
    )
    c0, x0 = core(own), across(own)
    row = lax.dynamic_slice_in_dim(block_table, me, 1, 0)

    (pair,) = in_vmem(
        fill,
        [pltpu.VMEM((2, rows, tokens), jnp.bfloat16)],
        [c0, pltpu.with_memory_space_constraint(half, pltpu.VMEM)],
        {1: 0},
    )
    z1 = along(pair, 1)
    queries_t = pltpu.with_memory_space_constraint(queries[0].T, pltpu.VMEM)

    def run(places, pieces, state, up=None, chosen=None):
        return stage(places, pieces, row, doc_ids, queries_t, state, up, sizes, chosen)

    state = run([(0, 0, 0)], [pair], None)
    *state, x0 = tie(*state, x0)
    cx0 = core(x0)
    state = run([(0, 1, 0)], [x0], state)
    *state, z1 = tie(*state, z1)
    z2, cz1, x1 = along(z1, 2), core(z1), across(z1)
    state = run([(0, 1, 1), (1, 0, 0)], [cx0, z1], state)
    *state, z2 = tie(*state, z2)
    z3, cz2 = along(z2, 3), core(z2)
    state = run([(1, 0, 1), (2, 0, 0)], [cz1, z2], state)
    *state, x1, z3 = tie(*state, x1, z3)
    x3, xz2, cx1, cz3 = across(z3), along(x1, 2), core(x1), core(z3)
    state = run([(2, 0, 1), (1, 1, 0), (3, 0, 0)], [cz2, x1, z3], state)
    *state, xz2 = tie(*state, xz2)
    cxz2 = core(xz2)
    state = run([(1, 1, 1), (3, 0, 1)], [cx1, cz3], state)
    *state, x3 = tie(*state, x3)
    cx3 = core(x3)
    state = run([(2, 1, 0), (2, 1, 1)], [xz2, cxz2], state)
    sections = lax.axis_size("section")
    handed = []
    for part in (tuple(range(heads - heads // 4)), tuple(range(heads - heads // 4, heads))):
        *state, heads_out = run(
            [(3, 1, 0), (3, 1, 1)], [x3, cx3], state, w_uv[0], part
        )
        handed.append(lax.ppermute(heads_out[None], "section", [(i, (i + 1) % sections) for i in range(sections)]))
    return jnp.concatenate(handed, axis=2)


def solution(mesh):
    placed = (
        P("section", "ctx", None),
        P("section", None, "ctx"),
        P("section", "ctx"),
        P(),
        P("section", None, None, None),
    )
    return jax.shard_map(
        shards, mesh=mesh, in_specs=placed, out_specs=P("section", "ctx", None), check_vma=False
    )
```

```python
import functools
import jax
import jax.numpy as jnp
from jax import lax
from jax.experimental import pallas as pl
from jax.experimental.pallas import tpu as pltpu
from jax.sharding import PartitionSpec as P

very_low = -1e30
log2_e = 1.4426950408889634
id_rows = 16
documents = 8


def dot(a, b, of_a, of_b):
    return lax.dot_general(a, b, (((of_a,), (of_b,)), ((), ())), preferred_element_type=jnp.float32)


def origin_of(me, place, e):
    step, across, swapped = place
    holder = me ^ (2 * across + swapped)
    if step == 0:
        return holder ^ e
    back = jnp.where((holder & 1) == 0, step, 7 - step)
    return (holder ^ e) - 4 * back


def attend(places, first, chosen, final, packs, factor_scale, row, ids_s, ids_v, queries, *refs):
    pieces, refs = refs[: len(places)], refs[len(places) :]
    if final:
        up, refs = refs[0], refs[1:]
    if not first:
        refs = refs[3:]
    if packs == "use":
        (keys, values, bias), refs = refs[:3], refs[3:]
    (peak, total, accum), refs = refs[:3], refs[3:]
    if final:
        out, refs = refs[0], refs[1:]
    if packs == "make":
        (keys, values, bias), refs = refs[:3], refs[3:]
    if not packs:
        (flipped, turned, values, bias), refs = refs[:4], refs[4:]
    score_buf, weight_buf, factor_buf = refs
    heads, latent, tokens = accum.shape
    width = queries.shape[0] // heads
    me = lax.axis_index("ctx")
    first_id = ids_s[0, 0]
    blocks = []
    for piece, place in zip(pieces, places):
        for e in range(piece.shape[0]):
            blocks.append((piece.at[e], place, e))
    if first:
        peak[...] = jnp.full(peak.shape, very_low, jnp.float32)
        total[...] = jnp.zeros(total.shape, jnp.float32)
        accum[...] = jnp.zeros(accum.shape, jnp.float32)
    query_ids = ids_v[...]
    key_at = lax.broadcasted_iota(jnp.int32, (tokens, tokens), 0)
    first_float = first_id.astype(jnp.float32)
    key_ids = [b[width : width + id_rows, :].astype(jnp.float32)[0:1, :] for b, _, _ in blocks]
    counts = [jnp.sum(jnp.where(k < first_float, 1.0, 0.0), axis=1, keepdims=True) for k in key_ids]
    befores = [c[0, 0].astype(jnp.int32) for c in counts]
    live_count = jnp.int32(0)
    for (block, place, e), ids_here, before in zip(blocks, key_ids, befores):
        own = place == (0, 0, 0) and e == 0
        origin = origin_of(me, place, e)
        if own:
            live = jnp.bool_(True)
        else:
            hit = row[0, jnp.maximum(origin, 0)]
            live = (origin >= 0) & (origin < me) & (hit == 1) & (before < tokens)

        def pack(block=block, ids_here=ids_here, before=before, slot=live_count, own=own):
            values[slot] = block[0:width, :]
            if packs:
                keys[slot] = block[0:width, :].T
            if own:
                start = jnp.zeros(query_ids.shape, jnp.int32)
                for d in range(documents):
                    below = jnp.sum(jnp.where(ids_here < float(d), 1.0, 0.0), axis=1, keepdims=True)
                    start = jnp.where(query_ids == d, below.astype(jnp.int32), start)
                query_at = lax.broadcasted_iota(jnp.int32, (tokens, tokens), 1)
                allowed = (key_at >= start) & (key_at <= query_at)
            else:
                allowed = (key_at >= before) & (query_ids == first_id)
            bias[slot] = jnp.where(allowed, 0.0, very_low)

        if own:
            pack()
        elif packs != "use":
            pl.when(live)(pack)
        live_count = live_count + live.astype(jnp.int32)

    spans = [slice(at, min(at + 128, width)) for at in range(0, width, 128)]
    count = len(chosen)
    shares = [spans[len(spans) * i // (count - 1) : len(spans) * (i + 1) // (count - 1)] for i in range(count - 1)]

    def score(slot, head, half):
        rows = queries[head * width : (head + 1) * width, :]
        turned_keys = keys[slot] if packs else flipped[...]
        score_buf[half] = dot(turned_keys, rows, 1, 0) + bias[slot]

    def weigh(head, half):
        scores = score_buf[half]
        old = peak[head : head + 1, :]
        new = jnp.maximum(old, jnp.max(scores, axis=0, keepdims=True))
        factor = jnp.exp2((old - new) * factor_scale)
        weights = jnp.exp2((scores - new) * factor_scale)
        total[head : head + 1, :] = total[head : head + 1, :] * factor + jnp.sum(weights, axis=0, keepdims=True)
        peak[head : head + 1, :] = new
        factor_buf[half] = jnp.broadcast_to(factor, factor_buf.shape[1:])
        weight_buf[half] = weights.astype(jnp.bfloat16)

    def mix(slot, head, half):
        accum[head] = accum[head] * factor_buf[half][0:1, :] + dot(values[slot, 0:latent, :], weight_buf[half], 1, 0)

    @pl.when(live_count > 0)
    def _():
        weight_buf[1] = jnp.zeros(weight_buf.shape[1:], weight_buf.dtype)
        factor_buf[1] = jnp.ones(factor_buf.shape[1:], factor_buf.dtype)
        if not packs:
            flipped[...] = values[0].T
        score(0, chosen[0], 0)

        def over_live(slot, carry):
            after, prior = jnp.minimum(slot + 1, live_count - 1), jnp.maximum(slot - 1, 0)
            for i, head in enumerate(chosen):
                half = i % 2
                if i == count - 1 and not packs:
                    flipped[...] = turned[...]
                score(slot if i < count - 1 else after, chosen[(i + 1) % count], 1 - half)
                weigh(head, half)
                mix(slot if i > 0 else prior, chosen[i - 1], 1 - half)
                if i < count - 1 and not packs:
                    for span in shares[i]:
                        turned[:, span] = values[after, span, :].T
            return carry

        lax.fori_loop(0, live_count, over_live, 0)
        mix(live_count - 1, chosen[-1], (count - 1) % 2)

    if final:
        value_width = up.shape[2]
        for i, head in enumerate(chosen):
            mixed = (accum[head] / total[head : head + 1, :]).astype(jnp.bfloat16)
            part = dot(up[head], mixed, 0, 0)
            out[:, i * value_width : (i + 1) * value_width] = part.T.astype(jnp.bfloat16)


def stage(places, pieces, row, ids, queries, state, up, sizes, chosen=None, packs=None):
    heads, latent, tokens, width, value_width = sizes
    first, final = state is None, up is not None
    chosen = tuple(range(heads)) if chosen is None else chosen
    count = sum(p.shape[0] for p in pieces)
    scalars, vectors = pl.BlockSpec(memory_space=pltpu.SMEM), pl.BlockSpec(memory_space=pltpu.VMEM)
    shapes = [((heads, tokens), jnp.float32), ((heads, tokens), jnp.float32), ((heads, latent, tokens), jnp.float32)]
    operands = [row, ids, ids, queries, *pieces]
    specs = [scalars, scalars, vectors, vectors] + [vectors] * len(pieces)
    aliases = {}
    out_shape = [pltpu.VMEM(shape, dtype) for shape, dtype in shapes]
    if final:
        operands.append(up)
        specs.append(vectors)
        out_shape.append(jax.ShapeDtypeStruct((tokens, len(chosen) * value_width), jnp.bfloat16))
    if not first:
        aliases = {len(operands) + i: i for i in range(3)}
        operands += [pltpu.with_memory_space_constraint(x, pltpu.VMEM) for x in state]
        specs += [vectors] * 3
    packed = [
        pltpu.VMEM((count, tokens, width), jnp.bfloat16),
        pltpu.VMEM((count, width, tokens), jnp.bfloat16),
        pltpu.VMEM((count, tokens, tokens), jnp.float32),
    ]
    scratch = []
    if packs == "make":
        out_shape += packed
    elif packs:
        operands += [pltpu.with_memory_space_constraint(x, pltpu.VMEM) for x in packs]
        specs += [vectors] * 3
        packs = "use"
    else:
        scratch = [pltpu.VMEM((tokens, width), jnp.bfloat16)] * 2 + packed[1:]
    scratch += [
        pltpu.VMEM((2, tokens, tokens), jnp.float32),
        pltpu.VMEM((2, tokens, tokens), jnp.bfloat16),
        pltpu.VMEM((2, 8, tokens), jnp.float32),
    ]
    scale = (value_width + width - latent) ** -0.5 * log2_e
    work = 2 * count * heads * tokens * tokens * (width + latent)
    result = pl.pallas_call(
        functools.partial(attend, tuple(places), first, chosen, final, packs, scale),
        out_shape=out_shape,
        in_specs=specs,
        out_specs=[vectors] * len(out_shape),
        scratch_shapes=scratch,
        input_output_aliases=aliases,
        cost_estimate=pl.CostEstimate(
            flops=work, bytes_accessed=count * 2 * width * tokens, transcendentals=count * heads * tokens * tokens
        ),
        compiler_params=pltpu.CompilerParams(vmem_limit_bytes=24 * 2**20),
        name="attend",
    )(*operands)
    return list(result)


def join(cache, ids, own, pair):
    width = cache.shape[1]
    rows = jnp.broadcast_to(ids[...].astype(jnp.float32), (id_rows, ids.shape[1])).astype(jnp.bfloat16)
    for out in (own, pair):
        out[0, 0:width, :] = cache[0]
        out[0, width : width + id_rows, :] = rows


def fill(other, half, pair):
    pair[1] = other[0]


def in_vmem(kernel, out_shape, operands, aliases):
    vectors = pl.BlockSpec(memory_space=pltpu.VMEM)
    return pl.pallas_call(
        kernel,
        out_shape=out_shape,
        in_specs=[vectors] * len(operands),
        out_specs=[vectors] * len(out_shape),
        input_output_aliases=aliases,
        compiler_params=pltpu.CompilerParams(vmem_limit_bytes=8 * 2**20),
    )(*operands)


def tie(*arrays):
    return list(lax.optimization_barrier(tuple(arrays)))


def shards(queries, latent_cache, doc_ids, block_table, w_uv):
    tokens, heads, latent, value_width = queries.shape[1], w_uv.shape[1], w_uv.shape[2], w_uv.shape[3]
    width = latent_cache.shape[1]
    sizes = (heads, latent, tokens, width, value_width)
    devices = lax.axis_size("ctx")
    me = lax.axis_index("ctx")

    def across(x):
        return lax.ppermute(x, "ctx", [(i, i ^ 2) for i in range(devices)])

    def core(x):
        return lax.ppermute(x, "ctx", [(i, i ^ 1) for i in range(devices)])

    def along(x, step):
        down = 8 if step == 1 else 4
        return lax.ppermute(x, "ctx", [(i, (i + 4 if i % 2 == 0 else i - down) % devices) for i in range(devices)])

    rows = width + id_rows
    own, half = in_vmem(
        join,
        [pltpu.VMEM((1, rows, tokens), jnp.bfloat16), pltpu.VMEM((2, rows, tokens), jnp.bfloat16)],
        [latent_cache, doc_ids],
        {},
    )
    c0, x0 = core(own), across(own)
    row = lax.dynamic_slice_in_dim(block_table, me, 1, 0)

    (pair,) = in_vmem(
        fill,
        [pltpu.VMEM((2, rows, tokens), jnp.bfloat16)],
        [c0, pltpu.with_memory_space_constraint(half, pltpu.VMEM)],
        {1: 0},
    )
    z1 = along(pair, 1)
    queries_t = pltpu.with_memory_space_constraint(queries[0].T, pltpu.VMEM)

    def run(places, pieces, state, up=None, chosen=None, packs=None):
        return stage(places, pieces, row, doc_ids, queries_t, state, up, sizes, chosen, packs)

    state = run([(0, 0, 0)], [pair], None)
    *state, x0 = tie(*state, x0)
    cx0 = core(x0)
    state = run([(0, 1, 0)], [x0], state)
    *state, z1 = tie(*state, z1)
    z2, cz1, x1 = along(z1, 2), core(z1), across(z1)
    state = run([(0, 1, 1), (1, 0, 0)], [cx0, z1], state)
    *state, z2 = tie(*state, z2)
    z3, cz2 = along(z2, 3), core(z2)
    state = run([(1, 0, 1), (2, 0, 0)], [cz1, z2], state)
    *state, x1, z3 = tie(*state, x1, z3)
    x3, xz2, cx1, cz3 = across(z3), along(x1, 2), core(x1), core(z3)
    state = run([(2, 0, 1), (1, 1, 0), (3, 0, 0)], [cz2, x1, z3], state)
    *state, xz2 = tie(*state, xz2)
    cxz2 = core(xz2)
    state = run([(1, 1, 1), (3, 0, 1)], [cx1, cz3], state)
    *state, x3 = tie(*state, x3)
    cx3 = core(x3)
    sections = lax.axis_size("section")

    def hand_on(x):
        return lax.ppermute(x[None], "section", [(i, (i + 1) % sections) for i in range(sections)])

    last = ([(2, 1, 0), (2, 1, 1), (3, 1, 0), (3, 1, 1)], [xz2, cxz2, x3, cx3])
    half, quarter = heads // 2, heads // 4
    parts = [tuple(range(half)), tuple(range(half, half + quarter)), tuple(range(half + quarter, heads))]
    *state, part, keys, values, bias = run(*last, state, w_uv[0], parts[0], "make")
    packs = [keys, values, bias]
    handed = [hand_on(part)]
    *state, part = run(*last, state, w_uv[0], parts[1], packs)
    handed.append(hand_on(part))
    *state, part = run(*last, state, w_uv[0], parts[2], packs)
    part, handed[1] = tie(part, handed[1])
    handed.append(hand_on(part))
    return jnp.concatenate(handed, axis=2)


def solution(mesh):
    placed = (
        P("section", "ctx", None),
        P("section", None, "ctx"),
        P("section", "ctx"),
        P(),
        P("section", None, None, None),
    )
    return jax.shard_map(
        shards, mesh=mesh, in_specs=placed, out_specs=P("section", "ctx", None), check_vma=False
    )
```

```python
import functools
import jax
import jax.numpy as jnp
from jax import lax
from jax.experimental import pallas as pl
from jax.experimental.pallas import tpu as pltpu
from jax.sharding import PartitionSpec as P

very_low = -1e30
log2_e = 1.4426950408889634
id_rows = 16
documents = 8


def dot(a, b, of_a, of_b):
    return lax.dot_general(a, b, (((of_a,), (of_b,)), ((), ())), preferred_element_type=jnp.float32)


def origin_of(me, place, e):
    step, across, swapped = place
    holder = me ^ (2 * across + swapped)
    if step == 0:
        return holder ^ e
    back = jnp.where((holder & 1) == 0, step, 7 - step)
    return (holder ^ e) - 4 * back


def attend(places, first, chosen, final, packs, factor_scale, row, ids_s, ids_v, queries, *refs):
    pieces, refs = refs[: len(places)], refs[len(places) :]
    if final:
        up, refs = refs[0], refs[1:]
    if not first:
        refs = refs[3:]
    if packs == "use":
        (keys, values, bias), refs = refs[:3], refs[3:]
    (peak, total, accum), refs = refs[:3], refs[3:]
    if final:
        out, refs = refs[0], refs[1:]
    if packs == "make":
        (keys, values, bias), refs = refs[:3], refs[3:]
    if not packs:
        (flipped, turned, values, bias), refs = refs[:4], refs[4:]
    score_buf, weight_buf, factor_buf = refs
    heads, latent, tokens = accum.shape
    width = queries.shape[0] // heads
    me = lax.axis_index("ctx")
    first_id = ids_s[0, 0]
    blocks = []
    for piece, place in zip(pieces, places):
        for e in range(piece.shape[0]):
            blocks.append((piece.at[e], place, e))
    if first:
        peak[...] = jnp.full(peak.shape, very_low, jnp.float32)
        total[...] = jnp.zeros(total.shape, jnp.float32)
        accum[...] = jnp.zeros(accum.shape, jnp.float32)
    query_ids = ids_v[...]
    key_at = lax.broadcasted_iota(jnp.int32, (tokens, tokens), 0)
    first_float = first_id.astype(jnp.float32)
    key_ids = [b[width : width + id_rows, :].astype(jnp.float32)[0:1, :] for b, _, _ in blocks]
    counts = [jnp.sum(jnp.where(k < first_float, 1.0, 0.0), axis=1, keepdims=True) for k in key_ids]
    befores = [c[0, 0].astype(jnp.int32) for c in counts]
    live_count = jnp.int32(0)
    for (block, place, e), ids_here, before in zip(blocks, key_ids, befores):
        own = place == (0, 0, 0) and e == 0
        origin = origin_of(me, place, e)
        if own:
            live = jnp.bool_(True)
        else:
            hit = row[0, jnp.maximum(origin, 0)]
            live = (origin >= 0) & (origin < me) & (hit == 1) & (before < tokens)

        def pack(block=block, ids_here=ids_here, before=before, slot=live_count, own=own):
            values[slot] = block[0:width, :]
            if packs:
                keys[slot] = block[0:width, :].T
            if own:
                start = jnp.zeros(query_ids.shape, jnp.int32)
                for d in range(documents):
                    below = jnp.sum(jnp.where(ids_here < float(d), 1.0, 0.0), axis=1, keepdims=True)
                    start = jnp.where(query_ids == d, below.astype(jnp.int32), start)
                query_at = lax.broadcasted_iota(jnp.int32, (tokens, tokens), 1)
                allowed = (key_at >= start) & (key_at <= query_at)
            else:
                allowed = (key_at >= before) & (query_ids == first_id)
            bias[slot] = jnp.where(allowed, 0.0, very_low)

        if own:
            pack()
        elif packs != "use":
            pl.when(live)(pack)
        live_count = live_count + live.astype(jnp.int32)

    spans = [slice(at, min(at + 128, width)) for at in range(0, width, 128)]
    count = len(chosen)
    shares = [spans[len(spans) * i // (count - 1) : len(spans) * (i + 1) // (count - 1)] for i in range(count - 1)]

    def score(slot, head, half):
        rows = queries[head * width : (head + 1) * width, :]
        turned_keys = keys[slot] if packs else flipped[...]
        score_buf[half] = dot(turned_keys, rows, 1, 0) + bias[slot]

    def weigh(head, half):
        scores = score_buf[half]
        old = peak[head : head + 1, :]
        new = jnp.maximum(old, jnp.max(scores, axis=0, keepdims=True))
        factor = jnp.exp2((old - new) * factor_scale)
        weights = jnp.exp2((scores - new) * factor_scale)
        total[head : head + 1, :] = total[head : head + 1, :] * factor + jnp.sum(weights, axis=0, keepdims=True)
        peak[head : head + 1, :] = new
        factor_buf[half] = jnp.broadcast_to(factor, factor_buf.shape[1:])
        weight_buf[half] = weights.astype(jnp.bfloat16)

    def mix(slot, head, half):
        accum[head] = accum[head] * factor_buf[half][0:1, :] + dot(values[slot, 0:latent, :], weight_buf[half], 1, 0)

    @pl.when(live_count > 0)
    def _():
        weight_buf[1] = jnp.zeros(weight_buf.shape[1:], weight_buf.dtype)
        factor_buf[1] = jnp.ones(factor_buf.shape[1:], factor_buf.dtype)
        if not packs:
            flipped[...] = values[0].T
        score(0, chosen[0], 0)

        def over_live(slot, carry):
            after, prior = jnp.minimum(slot + 1, live_count - 1), jnp.maximum(slot - 1, 0)
            for i, head in enumerate(chosen):
                half = i % 2
                if i == count - 1 and not packs:
                    flipped[...] = turned[...]
                score(slot if i < count - 1 else after, chosen[(i + 1) % count], 1 - half)
                weigh(head, half)
                mix(slot if i > 0 else prior, chosen[i - 1], 1 - half)
                if i < count - 1 and not packs:
                    for span in shares[i]:
                        turned[:, span] = values[after, span, :].T
            return carry

        lax.fori_loop(0, live_count, over_live, 0)
        mix(live_count - 1, chosen[-1], (count - 1) % 2)

    if final:
        value_width = up.shape[2]
        for i, head in enumerate(chosen):
            mixed = (accum[head] / total[head : head + 1, :]).astype(jnp.bfloat16)
            part = dot(up[head], mixed, 0, 0)
            out[:, i * value_width : (i + 1) * value_width] = part.T.astype(jnp.bfloat16)


def stage(places, pieces, row, ids, queries, state, up, sizes, chosen=None, packs=None):
    heads, latent, tokens, width, value_width = sizes
    first, final = state is None, up is not None
    chosen = tuple(range(heads)) if chosen is None else chosen
    count = sum(p.shape[0] for p in pieces)
    scalars, vectors = pl.BlockSpec(memory_space=pltpu.SMEM), pl.BlockSpec(memory_space=pltpu.VMEM)
    shapes = [((heads, tokens), jnp.float32), ((heads, tokens), jnp.float32), ((heads, latent, tokens), jnp.float32)]
    operands = [row, ids, ids, queries, *pieces]
    specs = [scalars, scalars, vectors, vectors] + [vectors] * len(pieces)
    aliases = {}
    out_shape = [pltpu.VMEM(shape, dtype) for shape, dtype in shapes]
    if final:
        operands.append(up)
        specs.append(vectors)
        out_shape.append(jax.ShapeDtypeStruct((tokens, len(chosen) * value_width), jnp.bfloat16))
    if not first:
        aliases = {len(operands) + i: i for i in range(3)}
        operands += [pltpu.with_memory_space_constraint(x, pltpu.VMEM) for x in state]
        specs += [vectors] * 3
    packed = [
        pltpu.VMEM((count, tokens, width), jnp.bfloat16),
        pltpu.VMEM((count, width, tokens), jnp.bfloat16),
        pltpu.VMEM((count, tokens, tokens), jnp.float32),
    ]
    scratch = []
    if packs == "make":
        out_shape += packed
    elif packs:
        operands += [pltpu.with_memory_space_constraint(x, pltpu.VMEM) for x in packs]
        specs += [vectors] * 3
        packs = "use"
    else:
        scratch = [pltpu.VMEM((tokens, width), jnp.bfloat16)] * 2 + packed[1:]
    scratch += [
        pltpu.VMEM((2, tokens, tokens), jnp.float32),
        pltpu.VMEM((2, tokens, tokens), jnp.bfloat16),
        pltpu.VMEM((2, 8, tokens), jnp.float32),
    ]
    scale = (value_width + width - latent) ** -0.5 * log2_e
    work = 2 * count * heads * tokens * tokens * (width + latent)
    result = pl.pallas_call(
        functools.partial(attend, tuple(places), first, chosen, final, packs, scale),
        out_shape=out_shape,
        in_specs=specs,
        out_specs=[vectors] * len(out_shape),
        scratch_shapes=scratch,
        input_output_aliases=aliases,
        cost_estimate=pl.CostEstimate(
            flops=work, bytes_accessed=count * 2 * width * tokens, transcendentals=count * heads * tokens * tokens
        ),
        compiler_params=pltpu.CompilerParams(vmem_limit_bytes=24 * 2**20),
        name="attend",
    )(*operands)
    return list(result)


def join(cache, ids, own, pair):
    width = cache.shape[1]
    rows = jnp.broadcast_to(ids[...].astype(jnp.float32), (id_rows, ids.shape[1])).astype(jnp.bfloat16)
    for out in (own, pair):
        out[0, 0:width, :] = cache[0]
        out[0, width : width + id_rows, :] = rows


def fill(other, half, pair):
    pair[1] = other[0]


def in_vmem(kernel, out_shape, operands, aliases):
    vectors = pl.BlockSpec(memory_space=pltpu.VMEM)
    return pl.pallas_call(
        kernel,
        out_shape=out_shape,
        in_specs=[vectors] * len(operands),
        out_specs=[vectors] * len(out_shape),
        input_output_aliases=aliases,
        compiler_params=pltpu.CompilerParams(vmem_limit_bytes=8 * 2**20),
    )(*operands)


def tie(*arrays):
    return list(lax.optimization_barrier(tuple(arrays)))


def shards(queries, latent_cache, doc_ids, block_table, w_uv):
    tokens, heads, latent, value_width = queries.shape[1], w_uv.shape[1], w_uv.shape[2], w_uv.shape[3]
    width = latent_cache.shape[1]
    sizes = (heads, latent, tokens, width, value_width)
    devices = lax.axis_size("ctx")
    me = lax.axis_index("ctx")

    def across(x):
        return lax.ppermute(x, "ctx", [(i, i ^ 2) for i in range(devices)])

    def core(x):
        return lax.ppermute(x, "ctx", [(i, i ^ 1) for i in range(devices)])

    def along(x, step):
        down = 8 if step == 1 else 4
        return lax.ppermute(x, "ctx", [(i, (i + 4 if i % 2 == 0 else i - down) % devices) for i in range(devices)])

    rows = width + id_rows
    own, half = in_vmem(
        join,
        [pltpu.VMEM((1, rows, tokens), jnp.bfloat16), pltpu.VMEM((2, rows, tokens), jnp.bfloat16)],
        [latent_cache, doc_ids],
        {},
    )
    c0, x0 = core(own), across(own)
    row = lax.dynamic_slice_in_dim(block_table, me, 1, 0)

    (pair,) = in_vmem(
        fill,
        [pltpu.VMEM((2, rows, tokens), jnp.bfloat16)],
        [c0, pltpu.with_memory_space_constraint(half, pltpu.VMEM)],
        {1: 0},
    )
    z1 = along(pair, 1)
    queries_t = pltpu.with_memory_space_constraint(queries[0].T, pltpu.VMEM)

    def run(places, pieces, state, up=None, chosen=None, packs=None):
        return stage(places, pieces, row, doc_ids, queries_t, state, up, sizes, chosen, packs)

    state = run([(0, 0, 0)], [pair], None)
    *state, x0 = tie(*state, x0)
    cx0 = core(x0)
    state = run([(0, 1, 0)], [x0], state)
    *state, z1 = tie(*state, z1)
    z2, cz1, x1 = along(z1, 2), core(z1), across(z1)
    state = run([(0, 1, 1), (1, 0, 0)], [cx0, z1], state)
    *state, z2 = tie(*state, z2)
    z3, cz2 = along(z2, 3), core(z2)
    state = run([(1, 0, 1), (2, 0, 0)], [cz1, z2], state)
    *state, x1, z3 = tie(*state, x1, z3)
    x3, xz2, cx1, cz3 = across(z3), along(x1, 2), core(x1), core(z3)
    state = run([(2, 0, 1), (1, 1, 0)], [cz2, x1], state)
    state = run([(1, 1, 1), (3, 0, 0)], [cx1, z3], state)
    *state, xz2, x3 = tie(*state, xz2, x3)
    cxz2, cx3 = core(xz2), core(x3)
    state = run([(3, 0, 1)], [cz3], state)
    sections = lax.axis_size("section")

    def hand_on(x):
        return lax.ppermute(x[None], "section", [(i, (i + 1) % sections) for i in range(sections)])

    last = ([(2, 1, 0), (2, 1, 1), (3, 1, 0), (3, 1, 1)], [xz2, cxz2, x3, cx3])
    early = heads - heads // 4
    parts = tuple(range(early)), tuple(range(early, heads))
    *state, part, keys, values, bias = run(*last, state, w_uv[0], parts[0], "make")
    handed = [hand_on(part)]
    *state, part = run(*last, state, w_uv[0], parts[1], [keys, values, bias])
    handed.append(hand_on(part))
    return jnp.concatenate(handed, axis=2)


def solution(mesh):
    placed = (
        P("section", "ctx", None),
        P("section", None, "ctx"),
        P("section", "ctx"),
        P(),
        P("section", None, None, None),
    )
    return jax.shard_map(
        shards, mesh=mesh, in_specs=placed, out_specs=P("section", "ctx", None), check_vma=False
    )
```

```python
import functools
import jax
import jax.numpy as jnp
from jax import lax
from jax.experimental import pallas as pl
from jax.experimental.pallas import tpu as pltpu
from jax.sharding import PartitionSpec as P

very_low = -1e30
log2_e = 1.4426950408889634
id_rows = 16
documents = 8


def dot(a, b, of_a, of_b):
    return lax.dot_general(a, b, (((of_a,), (of_b,)), ((), ())), preferred_element_type=jnp.float32)


def origin_of(me, place, e):
    step, across, swapped = place
    holder = me ^ (2 * across + swapped)
    if step == 0:
        return holder ^ e
    back = jnp.where((holder & 1) == 0, step, 7 - step)
    return (holder ^ e) - 4 * back


def attend(places, first, chosen, final, packs, factor_scale, row_v, ids_v, queries, *refs):
    pieces, refs = refs[: len(places)], refs[len(places) :]
    if final:
        up, refs = refs[0], refs[1:]
    if not first:
        refs = refs[3:]
    if packs == "use":
        (keys, values, bias), refs = refs[:3], refs[3:]
    (peak, total, accum), refs = refs[:3], refs[3:]
    if final:
        out, refs = refs[0], refs[1:]
    if packs == "make":
        (keys, values, bias), refs = refs[:3], refs[3:]
    if not packs:
        (flipped, turned, values, bias), refs = refs[:4], refs[4:]
    score_buf, weight_buf, factor_buf = refs
    heads, latent, tokens = accum.shape
    width = queries.shape[0] // heads
    me = lax.axis_index("ctx")
    row = row_v[...]
    block_at = lax.broadcasted_iota(jnp.int32, row.shape, 1)
    blocks = []
    for piece, place in zip(pieces, places):
        for e in range(piece.shape[0]):
            blocks.append((piece.at[e], place, e))
    if first:
        peak[...] = jnp.full(peak.shape, very_low, jnp.float32)
        total[...] = jnp.zeros(total.shape, jnp.float32)
        accum[...] = jnp.zeros(accum.shape, jnp.float32)
    query_ids = ids_v[...]
    first_id = query_ids[:, 0:1]
    key_at = lax.broadcasted_iota(jnp.int32, (tokens, tokens), 0)
    first_float = first_id.astype(jnp.float32)
    key_ids = [b[width : width + id_rows, :].astype(jnp.float32)[0:1, :] for b, _, _ in blocks]
    counts = [jnp.sum(jnp.where(k < first_float, 1.0, 0.0), axis=1, keepdims=True) for k in key_ids]
    origins = [origin_of(me, place, e) for _, place, e in blocks]
    hits = [jnp.sum(jnp.where(block_at == o, row, 0), axis=1, keepdims=True) for o in origins]
    barred = [jnp.where(h == 1, c.astype(jnp.int32), tokens) for h, c in zip(hits, counts)]
    barred = [x[0, 0] for x in barred]
    live_count = jnp.int32(0)
    for (block, place, e), ids_here, origin, before in zip(blocks, key_ids, origins, barred):
        own = place == (0, 0, 0) and e == 0
        if own:
            live = jnp.bool_(True)
        else:
            live = (origin >= 0) & (origin < me) & (before < tokens)

        def pack(block=block, ids_here=ids_here, before=before, slot=live_count, own=own):
            values[slot] = block[0:width, :]
            if packs:
                keys[slot] = block[0:width, :].T
            if own:
                start = jnp.zeros(query_ids.shape, jnp.int32)
                for d in range(documents):
                    below = jnp.sum(jnp.where(ids_here < float(d), 1.0, 0.0), axis=1, keepdims=True)
                    start = jnp.where(query_ids == d, below.astype(jnp.int32), start)
                query_at = lax.broadcasted_iota(jnp.int32, (tokens, tokens), 1)
                allowed = (key_at >= start) & (key_at <= query_at)
            else:
                allowed = (key_at >= before) & (query_ids == first_id)
            bias[slot] = jnp.where(allowed, 0.0, very_low)

        if own:
            pack()
        elif packs != "use":
            pl.when(live)(pack)
        live_count = live_count + live.astype(jnp.int32)

    spans = [slice(at, min(at + 128, width)) for at in range(0, width, 128)]
    count = len(chosen)
    shares = [spans[len(spans) * i // (count - 1) : len(spans) * (i + 1) // (count - 1)] for i in range(count - 1)]

    def score(slot, head, half):
        rows = queries[head * width : (head + 1) * width, :]
        turned_keys = keys[slot] if packs else flipped[...]
        score_buf[half] = dot(turned_keys, rows, 1, 0) + bias[slot]

    def weigh(head, half):
        scores = score_buf[half]
        old = peak[head : head + 1, :]
        new = jnp.maximum(old, jnp.max(scores, axis=0, keepdims=True))
        factor = jnp.exp2((old - new) * factor_scale)
        weights = jnp.exp2((scores - new) * factor_scale)
        total[head : head + 1, :] = total[head : head + 1, :] * factor + jnp.sum(weights, axis=0, keepdims=True)
        peak[head : head + 1, :] = new
        factor_buf[half] = jnp.broadcast_to(factor, factor_buf.shape[1:])
        weight_buf[half] = weights.astype(jnp.bfloat16)

    def mix(slot, head, half):
        accum[head] = accum[head] * factor_buf[half][0:1, :] + dot(values[slot, 0:latent, :], weight_buf[half], 1, 0)

    @pl.when(live_count > 0)
    def _():
        weight_buf[1] = jnp.zeros(weight_buf.shape[1:], weight_buf.dtype)
        factor_buf[1] = jnp.ones(factor_buf.shape[1:], factor_buf.dtype)
        if not packs:
            flipped[...] = values[0].T
        score(0, chosen[0], 0)

        def over_live(slot, carry):
            after, prior = jnp.minimum(slot + 1, live_count - 1), jnp.maximum(slot - 1, 0)
            for i, head in enumerate(chosen):
                half = i % 2
                if i == count - 1 and not packs:
                    flipped[...] = turned[...]
                score(slot if i < count - 1 else after, chosen[(i + 1) % count], 1 - half)
                weigh(head, half)
                mix(slot if i > 0 else prior, chosen[i - 1], 1 - half)
                if i < count - 1 and not packs:
                    for span in shares[i]:
                        turned[:, span] = values[after, span, :].T
            return carry

        lax.fori_loop(0, live_count, over_live, 0)
        mix(live_count - 1, chosen[-1], (count - 1) % 2)

    if final:
        value_width = up.shape[2]
        for i, head in enumerate(chosen):
            mixed = (accum[head] / total[head : head + 1, :]).astype(jnp.bfloat16)
            part = dot(up[head], mixed, 0, 0)
            out[:, i * value_width : (i + 1) * value_width] = part.T.astype(jnp.bfloat16)


def stage(places, pieces, row, ids, queries, state, up, sizes, chosen=None, packs=None):
    heads, latent, tokens, width, value_width = sizes
    first, final = state is None, up is not None
    chosen = tuple(range(heads)) if chosen is None else chosen
    count = sum(p.shape[0] for p in pieces)
    vectors = pl.BlockSpec(memory_space=pltpu.VMEM)
    shapes = [((heads, tokens), jnp.float32), ((heads, tokens), jnp.float32), ((heads, latent, tokens), jnp.float32)]
    operands = [row, ids, queries, *pieces]
    specs = [vectors, vectors, vectors] + [vectors] * len(pieces)
    aliases = {}
    out_shape = [pltpu.VMEM(shape, dtype) for shape, dtype in shapes]
    if final:
        operands.append(up)
        specs.append(vectors)
        out_shape.append(jax.ShapeDtypeStruct((tokens, len(chosen) * value_width), jnp.bfloat16))
    if not first:
        aliases = {len(operands) + i: i for i in range(3)}
        operands += [pltpu.with_memory_space_constraint(x, pltpu.VMEM) for x in state]
        specs += [vectors] * 3
    packed = [
        pltpu.VMEM((count, tokens, width), jnp.bfloat16),
        pltpu.VMEM((count, width, tokens), jnp.bfloat16),
        pltpu.VMEM((count, tokens, tokens), jnp.float32),
    ]
    scratch = []
    if packs == "make":
        out_shape += packed
    elif packs:
        operands += [pltpu.with_memory_space_constraint(x, pltpu.VMEM) for x in packs]
        specs += [vectors] * 3
        packs = "use"
    else:
        scratch = [pltpu.VMEM((tokens, width), jnp.bfloat16)] * 2 + packed[1:]
    scratch += [
        pltpu.VMEM((2, tokens, tokens), jnp.float32),
        pltpu.VMEM((2, tokens, tokens), jnp.bfloat16),
        pltpu.VMEM((2, 8, tokens), jnp.float32),
    ]
    scale = (value_width + width - latent) ** -0.5 * log2_e
    work = 2 * count * heads * tokens * tokens * (width + latent)
    result = pl.pallas_call(
        functools.partial(attend, tuple(places), first, chosen, final, packs, scale),
        out_shape=out_shape,
        in_specs=specs,
        out_specs=[vectors] * len(out_shape),
        scratch_shapes=scratch,
        input_output_aliases=aliases,
        cost_estimate=pl.CostEstimate(
            flops=work, bytes_accessed=count * 2 * width * tokens, transcendentals=count * heads * tokens * tokens
        ),
        compiler_params=pltpu.CompilerParams(vmem_limit_bytes=24 * 2**20),
        name="attend",
    )(*operands)
    return list(result)


def join(cache, ids, own, pair):
    width = cache.shape[1]
    rows = jnp.broadcast_to(ids[...].astype(jnp.float32), (id_rows, ids.shape[1])).astype(jnp.bfloat16)
    for out in (own, pair):
        out[0, 0:width, :] = cache[0]
        out[0, width : width + id_rows, :] = rows


def fill(other, half, pair):
    pair[1] = other[0]


def in_vmem(kernel, out_shape, operands, aliases):
    vectors = pl.BlockSpec(memory_space=pltpu.VMEM)
    return pl.pallas_call(
        kernel,
        out_shape=out_shape,
        in_specs=[vectors] * len(operands),
        out_specs=[vectors] * len(out_shape),
        input_output_aliases=aliases,
        compiler_params=pltpu.CompilerParams(vmem_limit_bytes=8 * 2**20),
    )(*operands)


def tie(*arrays):
    return list(lax.optimization_barrier(tuple(arrays)))


def shards(queries, latent_cache, doc_ids, block_table, w_uv):
    tokens, heads, latent, value_width = queries.shape[1], w_uv.shape[1], w_uv.shape[2], w_uv.shape[3]
    width = latent_cache.shape[1]
    sizes = (heads, latent, tokens, width, value_width)
    devices = lax.axis_size("ctx")
    me = lax.axis_index("ctx")

    def across(x):
        return lax.ppermute(x, "ctx", [(i, i ^ 2) for i in range(devices)])

    def core(x):
        return lax.ppermute(x, "ctx", [(i, i ^ 1) for i in range(devices)])

    def along(x, step):
        down = 8 if step == 1 else 4
        return lax.ppermute(x, "ctx", [(i, (i + 4 if i % 2 == 0 else i - down) % devices) for i in range(devices)])

    rows = width + id_rows
    own, half = in_vmem(
        join,
        [pltpu.VMEM((1, rows, tokens), jnp.bfloat16), pltpu.VMEM((2, rows, tokens), jnp.bfloat16)],
        [latent_cache, doc_ids],
        {},
    )
    c0, x0 = core(own), across(own)
    row = lax.dynamic_slice_in_dim(block_table, me, 1, 0)

    (pair,) = in_vmem(
        fill,
        [pltpu.VMEM((2, rows, tokens), jnp.bfloat16)],
        [c0, pltpu.with_memory_space_constraint(half, pltpu.VMEM)],
        {1: 0},
    )
    z1 = along(pair, 1)
    queries_t = pltpu.with_memory_space_constraint(queries[0].T, pltpu.VMEM)

    def run(places, pieces, state, up=None, chosen=None, packs=None):
        return stage(places, pieces, row, doc_ids, queries_t, state, up, sizes, chosen, packs)

    state = run([(0, 0, 0)], [pair], None)
    *state, x0 = tie(*state, x0)
    cx0 = core(x0)
    state = run([(0, 1, 0)], [x0], state)
    *state, z1 = tie(*state, z1)
    z2, cz1, x1 = along(z1, 2), core(z1), across(z1)
    state = run([(0, 1, 1), (1, 0, 0)], [cx0, z1], state)
    *state, z2 = tie(*state, z2)
    z3, cz2 = along(z2, 3), core(z2)
    state = run([(1, 0, 1), (2, 0, 0)], [cz1, z2], state)
    *state, x1, z3 = tie(*state, x1, z3)
    x3, xz2, cx1, cz3 = across(z3), along(x1, 2), core(x1), core(z3)
    state = run([(2, 0, 1), (1, 1, 0)], [cz2, x1], state)
    state = run([(1, 1, 1), (3, 0, 0)], [cx1, z3], state)
    *state, xz2, x3 = tie(*state, xz2, x3)
    cxz2, cx3 = core(xz2), core(x3)
    state = run([(3, 0, 1)], [cz3], state)
    sections = lax.axis_size("section")

    def hand_on(x):
        return lax.ppermute(x[None], "section", [(i, (i + 1) % sections) for i in range(sections)])

    last = ([(2, 1, 0), (2, 1, 1), (3, 1, 0), (3, 1, 1)], [xz2, cxz2, x3, cx3])
    early = heads - heads // 4
    parts = tuple(range(early)), tuple(range(early, heads))
    *state, part, keys, values, bias = run(*last, state, w_uv[0], parts[0], "make")
    handed = [hand_on(part)]
    *state, part = run(*last, state, w_uv[0], parts[1], [keys, values, bias])
    handed.append(hand_on(part))
    return jnp.concatenate(handed, axis=2)


def solution(mesh):
    placed = (
        P("section", "ctx", None),
        P("section", None, "ctx"),
        P("section", "ctx"),
        P(),
        P("section", None, None, None),
    )
    return jax.shard_map(
        shards, mesh=mesh, in_specs=placed, out_specs=P("section", "ctx", None), check_vma=False
    )
```

```python
import functools
import jax
import jax.numpy as jnp
from jax import lax
from jax.experimental import pallas as pl
from jax.experimental.pallas import tpu as pltpu
from jax.sharding import PartitionSpec as P

very_low = -1e30
log2_e = 1.4426950408889634
id_rows = 16
documents = 8


def dot(a, b, of_a, of_b):
    return lax.dot_general(a, b, (((of_a,), (of_b,)), ((), ())), preferred_element_type=jnp.float32)


def origin_of(me, place, e):
    step, across, swapped = place
    holder = me ^ (2 * across + swapped)
    if step == 0:
        return holder ^ e
    back = jnp.where((holder & 1) == 0, step, 7 - step)
    return (holder ^ e) - 4 * back


def attend(places, first, chosen, final, packs, factor_scale, row_v, ids_v, queries, *refs):
    pieces, refs = refs[: len(places)], refs[len(places) :]
    if final:
        up, refs = refs[0], refs[1:]
    if not first:
        refs = refs[3:]
    if packs == "use":
        (keys, values, bias), refs = refs[:3], refs[3:]
    (peak, total, accum), refs = refs[:3], refs[3:]
    if final:
        out, refs = refs[0], refs[1:]
    if packs == "make":
        (keys, values, bias), refs = refs[:3], refs[3:]
    if not packs:
        (flipped, turned, values, bias), refs = refs[:4], refs[4:]
    score_buf, weight_buf, factor_buf = refs
    heads, latent, tokens = accum.shape
    width = queries.shape[0] // heads
    me = lax.axis_index("ctx")
    row = row_v[...]
    block_at = lax.broadcasted_iota(jnp.int32, row.shape, 1)
    blocks = []
    for piece, place in zip(pieces, places):
        for e in range(piece.shape[0]):
            blocks.append((piece.at[e], place, e))
    if first:
        peak[...] = jnp.full(peak.shape, very_low, jnp.float32)
        total[...] = jnp.zeros(total.shape, jnp.float32)
        accum[...] = jnp.zeros(accum.shape, jnp.float32)
    query_ids = ids_v[...]
    first_id = query_ids[:, 0:1]
    key_at = lax.broadcasted_iota(jnp.int32, (tokens, tokens), 0)
    first_float = first_id.astype(jnp.float32)
    key_ids = [b[width : width + id_rows, :].astype(jnp.float32)[0:1, :] for b, _, _ in blocks]
    counts = [jnp.sum(jnp.where(k < first_float, 1.0, 0.0), axis=1, keepdims=True) for k in key_ids]
    origins = [origin_of(me, place, e) for _, place, e in blocks]
    hits = [jnp.sum(jnp.where(block_at == o, row, 0), axis=1, keepdims=True) for o in origins]
    barred = [jnp.where(h == 1, c.astype(jnp.int32), tokens) for h, c in zip(hits, counts)]
    barred = [x[0, 0] for x in barred]
    live_count = jnp.int32(0)
    for (block, place, e), ids_here, origin, before in zip(blocks, key_ids, origins, barred):
        own = place == (0, 0, 0) and e == 0
        if own:
            live = jnp.bool_(True)
        else:
            live = (origin >= 0) & (origin < me) & (before < tokens)

        def pack(block=block, ids_here=ids_here, before=before, slot=live_count, own=own):
            values[slot] = block[0:width, :]
            if packs:
                keys[slot] = block[0:width, :].T
            if own:
                start = jnp.zeros(query_ids.shape, jnp.int32)
                for d in range(documents):
                    below = jnp.sum(jnp.where(ids_here < float(d), 1.0, 0.0), axis=1, keepdims=True)
                    start = jnp.where(query_ids == d, below.astype(jnp.int32), start)
                query_at = lax.broadcasted_iota(jnp.int32, (tokens, tokens), 1)
                allowed = (key_at >= start) & (key_at <= query_at)
            else:
                allowed = (key_at >= before) & (query_ids == first_id)
            bias[slot] = jnp.where(allowed, 0.0, very_low)

        if own:
            pack()
        elif packs != "use":
            pl.when(live)(pack)
        live_count = live_count + live.astype(jnp.int32)

    spans = [slice(at, min(at + 128, width)) for at in range(0, width, 128)]
    count = len(chosen)
    shares = [spans[len(spans) * i // (count - 1) : len(spans) * (i + 1) // (count - 1)] for i in range(count - 1)]

    def score(slot, head, half):
        rows = queries[head * width : (head + 1) * width, :]
        turned_keys = keys[slot] if packs else flipped[...]
        score_buf[half] = dot(turned_keys, rows, 1, 0) + bias[slot]

    def weigh(head, half):
        scores = score_buf[half]
        old = peak[head : head + 1, :]
        new = jnp.maximum(old, jnp.max(scores, axis=0, keepdims=True))
        factor = jnp.exp2((old - new) * factor_scale)
        weights = jnp.exp2((scores - new) * factor_scale)
        total[head : head + 1, :] = total[head : head + 1, :] * factor + jnp.sum(weights, axis=0, keepdims=True)
        peak[head : head + 1, :] = new
        factor_buf[half] = jnp.broadcast_to(factor, factor_buf.shape[1:])
        weight_buf[half] = weights.astype(jnp.bfloat16)

    def mix(slot, head, half):
        accum[head] = accum[head] * factor_buf[half][0:1, :] + dot(values[slot, 0:latent, :], weight_buf[half], 1, 0)

    @pl.when(live_count > 0)
    def _():
        weight_buf[1] = jnp.zeros(weight_buf.shape[1:], weight_buf.dtype)
        factor_buf[1] = jnp.ones(factor_buf.shape[1:], factor_buf.dtype)
        if not packs:
            flipped[...] = values[0].T
        score(0, chosen[0], 0)

        def over_live(slot, carry):
            after, prior = jnp.minimum(slot + 1, live_count - 1), jnp.maximum(slot - 1, 0)
            for i, head in enumerate(chosen):
                half = i % 2
                if i == count - 1 and not packs:
                    flipped[...] = turned[...]
                score(slot if i < count - 1 else after, chosen[(i + 1) % count], 1 - half)
                weigh(head, half)
                mix(slot if i > 0 else prior, chosen[i - 1], 1 - half)
                if i < count - 1 and not packs:
                    for span in shares[i]:
                        turned[:, span] = values[after, span, :].T
            return carry

        lax.fori_loop(0, live_count, over_live, 0)
        mix(live_count - 1, chosen[-1], (count - 1) % 2)

    if final:
        value_width = up.shape[2]
        for i, head in enumerate(chosen):
            mixed = (accum[head] / total[head : head + 1, :]).astype(jnp.bfloat16)
            part = dot(up[head], mixed, 0, 0)
            out[:, i * value_width : (i + 1) * value_width] = part.T.astype(jnp.bfloat16)


def stage(places, pieces, row, ids, queries, state, up, sizes, chosen=None, packs=None):
    heads, latent, tokens, width, value_width = sizes
    first, final = state is None, up is not None
    chosen = tuple(range(heads)) if chosen is None else chosen
    count = sum(p.shape[0] for p in pieces)
    vectors = pl.BlockSpec(memory_space=pltpu.VMEM)
    shapes = [((heads, tokens), jnp.float32), ((heads, tokens), jnp.float32), ((heads, latent, tokens), jnp.float32)]
    operands = [row, ids, queries, *pieces]
    specs = [vectors, vectors, vectors] + [vectors] * len(pieces)
    aliases = {}
    out_shape = [pltpu.VMEM(shape, dtype) for shape, dtype in shapes]
    if final:
        operands.append(up)
        specs.append(vectors)
        out_shape.append(jax.ShapeDtypeStruct((tokens, len(chosen) * value_width), jnp.bfloat16))
    if not first:
        aliases = {len(operands) + i: i for i in range(3)}
        operands += [pltpu.with_memory_space_constraint(x, pltpu.VMEM) for x in state]
        specs += [vectors] * 3
    packed = [
        pltpu.VMEM((count, tokens, width), jnp.bfloat16),
        pltpu.VMEM((count, width, tokens), jnp.bfloat16),
        pltpu.VMEM((count, tokens, tokens), jnp.float32),
    ]
    scratch = []
    if packs == "make":
        out_shape += packed
    elif packs:
        operands += [pltpu.with_memory_space_constraint(x, pltpu.VMEM) for x in packs]
        specs += [vectors] * 3
        packs = "use"
    else:
        scratch = [pltpu.VMEM((tokens, width), jnp.bfloat16)] * 2 + packed[1:]
    scratch += [
        pltpu.VMEM((2, tokens, tokens), jnp.float32),
        pltpu.VMEM((2, tokens, tokens), jnp.bfloat16),
        pltpu.VMEM((2, 8, tokens), jnp.float32),
    ]
    scale = (value_width + width - latent) ** -0.5 * log2_e
    work = 2 * count * heads * tokens * tokens * (width + latent)
    result = pl.pallas_call(
        functools.partial(attend, tuple(places), first, chosen, final, packs, scale),
        out_shape=out_shape,
        in_specs=specs,
        out_specs=[vectors] * len(out_shape),
        scratch_shapes=scratch,
        input_output_aliases=aliases,
        cost_estimate=pl.CostEstimate(
            flops=work, bytes_accessed=count * 2 * width * tokens, transcendentals=count * heads * tokens * tokens
        ),
        compiler_params=pltpu.CompilerParams(vmem_limit_bytes=24 * 2**20),
        name="attend",
    )(*operands)
    return list(result)


def join(cache, ids, own, pair):
    width = cache.shape[1]
    rows = jnp.broadcast_to(ids[...].astype(jnp.float32), (id_rows, ids.shape[1])).astype(jnp.bfloat16)
    for out in (own, pair):
        out[0, 0:width, :] = cache[0]
        out[0, width : width + id_rows, :] = rows


def fill(other, half, pair):
    pair[1] = other[0]


def in_vmem(kernel, out_shape, operands, aliases):
    vectors = pl.BlockSpec(memory_space=pltpu.VMEM)
    return pl.pallas_call(
        kernel,
        out_shape=out_shape,
        in_specs=[vectors] * len(operands),
        out_specs=[vectors] * len(out_shape),
        input_output_aliases=aliases,
        compiler_params=pltpu.CompilerParams(vmem_limit_bytes=8 * 2**20),
    )(*operands)


def tie(*arrays):
    return list(lax.optimization_barrier(tuple(arrays)))


def shards(queries, latent_cache, doc_ids, block_table, w_uv):
    tokens, heads, latent, value_width = queries.shape[1], w_uv.shape[1], w_uv.shape[2], w_uv.shape[3]
    width = latent_cache.shape[1]
    sizes = (heads, latent, tokens, width, value_width)
    devices = lax.axis_size("ctx")
    me = lax.axis_index("ctx")

    def across(x):
        return lax.ppermute(x, "ctx", [(i, i ^ 2) for i in range(devices)])

    def core(x):
        return lax.ppermute(x, "ctx", [(i, i ^ 1) for i in range(devices)])

    def along(x, step):
        down = 8 if step == 1 else 4
        return lax.ppermute(x, "ctx", [(i, (i + 4 if i % 2 == 0 else i - down) % devices) for i in range(devices)])

    rows = width + id_rows
    own, half = in_vmem(
        join,
        [pltpu.VMEM((1, rows, tokens), jnp.bfloat16), pltpu.VMEM((2, rows, tokens), jnp.bfloat16)],
        [latent_cache, doc_ids],
        {},
    )
    c0, x0 = core(own), across(own)
    row = lax.dynamic_slice_in_dim(block_table, me, 1, 0)

    (pair,) = in_vmem(
        fill,
        [pltpu.VMEM((2, rows, tokens), jnp.bfloat16)],
        [c0, pltpu.with_memory_space_constraint(half, pltpu.VMEM)],
        {1: 0},
    )
    z1 = along(pair, 1)
    queries_t = pltpu.with_memory_space_constraint(queries[0].T, pltpu.VMEM)

    def run(places, pieces, state, up=None, chosen=None, packs=None):
        return stage(places, pieces, row, doc_ids, queries_t, state, up, sizes, chosen, packs)

    state = run([(0, 0, 0)], [pair], None)
    *state, x0 = tie(*state, x0)
    cx0 = core(x0)
    state = run([(0, 1, 0)], [x0], state)
    *state, z1 = tie(*state, z1)
    z2, cz1, x1 = along(z1, 2), core(z1), across(z1)
    state = run([(0, 1, 1), (1, 0, 0)], [cx0, z1], state)
    *state, z2 = tie(*state, z2)
    z3, cz2 = along(z2, 3), core(z2)
    state = run([(1, 0, 1), (2, 0, 0)], [cz1, z2], state)
    *state, x1, z3 = tie(*state, x1, z3)
    x3, xz2, cx1, cz3 = across(z3), along(x1, 2), core(x1), core(z3)
    state = run([(2, 0, 1), (1, 1, 0)], [cz2, x1], state)
    *state, xz2 = tie(*state, xz2)
    cxz2 = core(xz2)
    state = run([(1, 1, 1), (3, 0, 0)], [cx1, z3], state)
    state = run([(3, 0, 1), (2, 1, 0)], [cz3, xz2], state)
    *state, x3 = tie(*state, x3)
    cx3 = core(x3)
    state = run([(2, 1, 1)], [cxz2], state)
    sections = lax.axis_size("section")

    def hand_on(x):
        return lax.ppermute(x[None], "section", [(i, (i + 1) % sections) for i in range(sections)])

    last = ([(3, 1, 0), (3, 1, 1)], [x3, cx3])
    early = heads - heads // 4
    parts = tuple(range(early)), tuple(range(early, heads))
    *state, part, keys, values, bias = run(*last, state, w_uv[0], parts[0], "make")
    handed = [hand_on(part)]
    *state, part = run(*last, state, w_uv[0], parts[1], [keys, values, bias])
    handed.append(hand_on(part))
    return jnp.concatenate(handed, axis=2)


def solution(mesh):
    placed = (
        P("section", "ctx", None),
        P("section", None, "ctx"),
        P("section", "ctx"),
        P(),
        P("section", None, None, None),
    )
    return jax.shard_map(
        shards, mesh=mesh, in_specs=placed, out_specs=P("section", "ctx", None), check_vma=False
    )
```
